32 devices in a mesh: row: 8 (over z, y), col: 4 (over x, core).
Axes of the slice: x: 2, y: 2, z: 4, core: 2. Of those that a mesh axis runs over, the one named last changes fastest.
Arguments:
- feats: bfloat16 [64, 64, 128], P(('row', 'col')), may hold values from -6 to 6
- coords: bfloat16 [64, 3, 128], P(('row', 'col')), may hold values from 0 to 1
- valid: int32 [64, 128], P(('row', 'col')), may hold values 0 or 1
- pairs: int32 [8, 4, 8, 2], P('row', 'col'), may hold values from 0 to 15, as said below
- pair_count: int32 [8, 4], P('row', 'col'), may hold values from 1 to 8, as said below
- w_first: bfloat16 [128, 128], replicated, may hold values from -0.5 to 0.5
- bias_first: float32 [128], replicated, may hold values from -3 to 3
- dist_scale: float32 [128], replicated, may hold values from -3 to 3
- w_second: bfloat16 [64, 128], replicated, may hold values from -0.5 to 0.5
- bias_second: float32 [64], replicated, may hold values from -3 to 3
- cotangent: bfloat16 [64, 64, 128], P(('row', 'col')), may hold values from -6 to 6
Outputs:
- updated: bfloat16 [64, 64, 128], P(('row', 'col'))
- grad_feats: float32 [64, 64, 128], P(('row', 'col'))
- grad_first: float32 [128, 128], replicated
- grad_bias_first: float32 [128], replicated
- grad_dist: float32 [128], replicated
- grad_second: float32 [64, 128], replicated
- grad_bias_second: float32 [64], replicated
The draws below stay inside these ranges and needn't reach their ends.
Inputs may be any that keep to these rules, and one draw needn't show every extreme that they name: pairs[r, c, p, 0] names a cell of row block r by its place, below 8; pairs[r, c, p, 1] a cell of column block c by its place, below 16. `pair_count`: some grid position has all 8 pairs live.
All inputs are finite; a program needn't handle non-finite values. No bound on the sum of `valid` on one device may be relied on, other than what follows from the above.
Results may differ from the reference program's by a relative error of at most 0.0045.
Values may be sent and summed in bfloat16 or wider, within the bound.
No kernel may reach another device: no remote copies, remote signals or barrier semaphores. Data moves between devices by JAX's collectives and lax.ppermute only.
A program may use at most 64 MiB of HBM per device.

```python
import jax
import jax.numpy as jnp
from jax import lax

L = 64
H = 128
CP = 128
CELL_DEV = 2
PAIRS = 8
ROW_BLOCK = 8
NC = 64
N_ROW = 8
N_COL = 4


def draw_pairs(key, part):
    base = jax.random.fold_in(key, 3)
    first_key, second_key = jax.random.split(base)
    firsts = jax.random.randint(first_key, (N_ROW, N_COL, PAIRS, 1), 0, CELL_DEV * N_COL)
    seconds = jax.random.randint(second_key, (N_ROW, N_COL, PAIRS, 1), 0, CELL_DEV * N_ROW)
    return jnp.concatenate([firsts, seconds], axis=3).astype(jnp.int32)


def draw_pair_count(key, part):
    base = jax.random.fold_in(key, 7)
    load_key, spot_key = jax.random.split(base)
    draws = jax.random.randint(load_key, (N_ROW * N_COL,), 0, PAIRS)
    counts = 1 + draws * draws // PAIRS
    spot = jax.random.randint(spot_key, (), 0, N_ROW * N_COL)
    counts = jnp.where(jnp.arange(N_ROW * N_COL) == spot, PAIRS, counts)
    return counts.reshape(N_ROW, N_COL).astype(jnp.int32)


def set_ends(result, own_key, smallest, high):
    dims = result.shape
    place = [jax.random.randint(jax.random.fold_in(own_key, axis), (), 0, dims[axis]) for axis in range(len(dims))]
    result = result.at[tuple(place)].set(smallest)
    longest = dims.index(max(dims))
    place[longest] = (place[longest] + 1) % dims[longest]
    return result.at[tuple(place)].set(high)


def block_scale(own_key, dims, shards, low, high):
    level = 1.0
    for position, shards_of in shards:
        steps = jax.random.uniform(jax.random.fold_in(jax.random.fold_in(own_key, 6), position), (shards_of,), jnp.float32, low / len(shards), high / len(shards))
        level = level * jnp.repeat(jnp.exp(steps), dims[position] // shards_of).reshape((-1,) + (1,) * (len(dims) - 1 - position))
    return level


def noise(key, extent, deviation, bound, cuts=(), kind=jnp.bfloat16):
    values = jax.random.normal(key, extent, jnp.float32) * deviation
    if len(cuts) > 0:
        values = block_scale(key, extent, cuts, -0.22, 0.18) * values
    return jnp.clip(values, min=-bound, max=bound).astype(kind)


def setup_inputs(seed: int = 0) -> dict:
    key_of = jax.random.split(jax.random.key(seed), 12)
    return {
        "feats": noise(key_of[0], (NC, L, CP), 1.0, 6.0, ((0, 32),)),
        "coords": jnp.clip(1.0 * jax.random.uniform(key_of[1], (NC, 3, CP), jnp.float32) ** block_scale(key_of[1], (NC, 3, CP), ((0, 32),), -0.2, 0.2), 0.0, 1.0).astype(jnp.bfloat16),
        "valid": set_ends((jax.random.randint(key_of[2], (NC, CP), 0, 8) < 7).astype(jnp.int32), jax.random.fold_in(key_of[2], 1), 0, 1),
        "pairs": draw_pairs(jax.random.fold_in(key_of[11], 71), 0),
        "pair_count": draw_pair_count(jax.random.fold_in(key_of[11], 71), 0),
        "w_first": noise(key_of[5], (H, 2 * L), (2 * L) ** -0.5, 0.5),
        "bias_first": noise(key_of[6], (H,), 0.5, 3.0, (), jnp.float32),
        "dist_scale": noise(key_of[7], (H,), 1.0, 3.0, (), jnp.float32),
        "w_second": noise(key_of[8], (L, H), H ** -0.5, 0.5),
        "bias_second": noise(key_of[9], (L,), 0.5, 3.0, (), jnp.float32),
        "cotangent": noise(key_of[10], (NC, L, CP), 1.0, 6.0, ((0, 32),)),
    }


def contract(spec, left, right):
    return jnp.einsum(spec, left.astype(jnp.float32), right.astype(jnp.float32), precision=lax.Precision.HIGHEST)


def silu_slope(value):
    sigm = jax.nn.sigmoid(value)
    return sigm * (1.0 + value * (1.0 - sigm))


def tile_terms(proj_row, proj_col, pos_row, pos_col, mask_row, mask_col, grad_row, w_second, bias_first, dist_scale, bias_second):
    offsets = pos_row[:, :, None] - pos_col[:, None, :]
    sq_dist = jnp.sum(offsets * offsets, axis=0)
    pre_hidden = proj_row[:, :, None] + proj_col[:, None, :] + dist_scale[:, None, None] * sq_dist[None] + bias_first[:, None, None]
    hidden = jax.nn.silu(pre_hidden).astype(jnp.bfloat16)
    pre_message = contract("mh,hij->mij", w_second, hidden) + bias_second[:, None, None]
    message = jax.nn.silu(pre_message)
    envelope = mask_row[:, None] * mask_col[None, :] / (1.0 + sq_dist) / CP
    gathered_msg = jnp.sum(envelope[None] * message, axis=2)
    grad_outer = envelope[None] * grad_row[:, :, None] * silu_slope(pre_message)
    grad_low = grad_outer.astype(jnp.bfloat16)
    grad_w2 = contract("mij,hij->mh", grad_low, hidden)
    grad_b2 = jnp.sum(grad_outer, axis=(1, 2))
    grad_hidden = contract("mh,mij->hij", w_second, grad_low)
    grad_inner = grad_hidden * silu_slope(pre_hidden)
    return (gathered_msg, jnp.sum(grad_inner, axis=2), jnp.sum(grad_inner, axis=1), grad_w2, grad_b2,
            jnp.sum(grad_inner * sq_dist[None], axis=(1, 2)), jnp.sum(grad_inner, axis=(1, 2)))


def reference(feats, coords, valid, pairs, pair_count, w_first, bias_first, dist_scale, w_second, bias_second, cotangent):
    feat_full = feats.astype(jnp.float32)
    proj_a = contract("hl,clp->chp", w_first[:, :L], feats)
    proj_b = contract("hl,clp->chp", w_first[:, L:], feats)
    positions = coords.astype(jnp.float32)
    mask_full = valid.astype(jnp.float32)
    grad_full = cotangent.astype(jnp.float32)

    def visit(state, index):
        row_pos = index // (N_COL * PAIRS)
        col_pos = (index // PAIRS) % N_COL
        tile = index % PAIRS
        row_cell = (row_pos * ROW_BLOCK + pairs[row_pos, col_pos, tile, 0]).astype(jnp.int32)
        local_col = pairs[row_pos, col_pos, tile, 1]
        col_cell = ((local_col // CELL_DEV) * ROW_BLOCK + col_pos * CELL_DEV + local_col % CELL_DEV).astype(jnp.int32)

        def work(inner):
            terms = tile_terms(proj_a[row_cell], proj_b[col_cell], positions[row_cell], positions[col_cell],
                               mask_full[row_cell], mask_full[col_cell], grad_full[row_cell],
                               w_second, bias_first, dist_scale, bias_second)
            return (inner[0].at[row_cell].add(terms[0]), inner[1].at[row_cell].add(terms[1]),
                    inner[2].at[col_cell].add(terms[2]), inner[3] + terms[3], inner[4] + terms[4],
                    inner[5] + terms[5], inner[6] + terms[6])

        return lax.cond(tile < pair_count[row_pos, col_pos], work, lambda inner: inner, state), None

    start = (jnp.zeros((NC, L, CP), jnp.float32), jnp.zeros((NC, H, CP), jnp.float32),
             jnp.zeros((NC, H, CP), jnp.float32), jnp.zeros((L, H), jnp.float32),
             jnp.zeros((L,), jnp.float32), jnp.zeros((H,), jnp.float32), jnp.zeros((H,), jnp.float32))
    final, unused = lax.scan(visit, start, jnp.arange(N_ROW * N_COL * PAIRS, dtype=jnp.int32))
    agg, grad_rows, grad_cols, grad_w2, grad_b2, grad_ds, grad_b1 = final
    updated = (feat_full + agg).astype(jnp.bfloat16)
    grad_feats = grad_full + contract("hl,chp->clp", w_first[:, :L], grad_rows) + contract("hl,chp->clp", w_first[:, L:], grad_cols)
    grad_first = jnp.concatenate([contract("chp,clp->hl", grad_rows, feats), contract("chp,clp->hl", grad_cols, feats)], axis=1)
    return updated, grad_feats, grad_first, grad_b1, grad_ds, grad_w2, grad_b2
```

```python
import functools
import jax
import jax.numpy as jnp
from jax import lax
from jax.experimental import pallas as pl
from jax.experimental.pallas import tpu as pltpu
from jax.sharding import PartitionSpec as P

L = 64
H = 128
CP = 128
GROUP = 16
WIDE = GROUP * CP
CELLS = 2
NT = (((1,), (1,)), ((), ()))
NN = (((1,), (0,)), ((), ()))
F32 = jnp.float32
BF16 = jnp.bfloat16


def dot(a, b, dims=NN):
    return lax.dot_general(a, b, dims, preferred_element_type=F32)


def split(value):
    high = value.astype(BF16)
    return high, (value - high.astype(F32)).astype(BF16)


def dot_split(a, b, dims=NN):
    high, low = split(b)
    return dot(a, high, dims) + dot(a, low, dims)


def column(row, rows):
    return jnp.transpose(jnp.broadcast_to(row, (rows, row.shape[1])))


def pair_kernel(
    count_ref, pairs_ref,
    r_ref, c_ref,
    w1_ref, b1_ref, ds_ref, w2_ref, b2_ref,
    rows_ref, cola_ref, colb_ref, par_ref,
    lhs, rhs, sums_lhs, sq_s, env_s, base_s, y_s, slope_s, x3_s,
    racc, cacc, gcol, gw2, gds,
):
    n_row = r_ref.shape[0]
    n_col = c_ref.shape[0]
    me_row, me_col = lax.axis_index("row"), lax.axis_index("col")
    halves = n_col // (2 * CELLS)
    ring = n_row // CELLS

    def place(cell):
        source, inner = cell // CELLS, cell % CELLS
        step = lax.rem(source // 2 - me_row // 2 + halves, halves)
        return (step * 2 + lax.rem(source + me_row, 2)) * CELLS + inner

    lane = lax.broadcasted_iota(jnp.int32, (H, CP), 1)
    onehot = (
        lax.broadcasted_iota(jnp.int32, (GROUP, WIDE), 1) // CP
        == lax.broadcasted_iota(jnp.int32, (GROUP, WIDE), 0)
    ).astype(F32)
    hot = onehot.astype(BF16)
    rhs[0:GROUP, :] = hot
    rhs[GROUP:2 * GROUP, :] = hot
    rhs[2 * GROUP:3 * GROUP, :] = jnp.zeros((GROUP, WIDE), BF16)
    rhs[3 * GROUP:4 * GROUP, :] = hot
    sums_lhs[0:GROUP, :] = hot
    sums_lhs[GROUP:2 * GROUP, :] = jnp.zeros((GROUP, WIDE), BF16)
    racc[...] = jnp.zeros_like(racc)
    cacc[...] = jnp.zeros_like(cacc)
    gw2[...] = jnp.zeros_like(gw2)
    gds[...] = jnp.zeros_like(gds)
    b1_b = column(b1_ref[...], CP)
    ds_b = 0.5 * column(ds_ref[...], CP)
    b2_b = 0.5 * jnp.transpose(jnp.broadcast_to(b2_ref[...], (CP, 2 * L))[:, :])[:L, :]
    ds_hi = ds_b.astype(BF16).astype(F32)
    ds_lo = ds_b - ds_hi
    ds_part = jnp.where(lane < 34, ds_hi, jnp.where(lane < 35, ds_lo, 0.0))
    w1 = w1_ref[...]
    w1r = w1[:, :L]
    w1c = w1[:, L:]
    w2 = w2_ref[...]
    w2h = (0.5 * w2.astype(F32)).astype(BF16)
    w2t = jnp.transpose(0.5 * w2.astype(F32)).astype(BF16)

    def tile(index, carry):
        u = pairs_ref[index, 0]
        v = place(pairs_ref[index, 1])
        a = 0.5 * (dot(w1r, r_ref[u, 0:L, :]) + b1_b)
        base_s[...] = 0.5 * dot(w1c, c_ref[v, 0:L, :])
        a_hi = a.astype(BF16).astype(F32)
        a_lo = a - a_hi
        cot = 0.5 * r_ref[u, L:2 * L, :].astype(F32)
        for g in range(CP // GROUP):
            hi_g = pltpu.roll(a_hi, (CP - GROUP * g) % CP, 1)
            lo_g = pltpu.roll(a_lo, (CP + GROUP - GROUP * g) % CP, 1)
            lhs[g, 0:H, :] = jnp.where(lane < 16, hi_g, jnp.where(lane < 32, lo_g, ds_part))[:, :64].astype(BF16)
            co_g = pltpu.roll(cot, (CP + 48 - GROUP * g) % CP, 1)
            lhs[g, H:H + L, :] = jnp.where((lane[:L] >= 48) & (lane[:L] < 64), co_g, 0.0)[:, :64].astype(BF16)
        xu = r_ref[u, 2 * L:2 * L + 16, :].astype(F32)
        xv = c_ref[v, L:L + 16, :].astype(F32)
        sq = jnp.zeros((CP, CP), F32)
        for k in range(3):
            off = column(xu[k:k + 1, :], CP) - xv[k:k + 1, :]
            sq = sq + off * off
        sq_s[...] = sq
        mu = column(xu[3:4, :], CP)
        mv = xv[3:4, :]
        env_s[...] = mu * mv / ((1.0 + sq) * CP)
        gcol[...] = jnp.zeros_like(gcol)

        def group(g, carry):
            first = pl.multiple_of(g * GROUP, GROUP)
            flat = jnp.concatenate(
                [sq_s[pl.ds(first + i, 1), :] for i in range(GROUP)], axis=1
            )
            flat_hi = flat.astype(BF16).astype(F32)
            flat_lo = flat - flat_hi
            sub = lax.broadcasted_iota(jnp.int32, (GROUP, WIDE), 0)
            block = jnp.where(
                (sub == 0) | (sub == 2), flat_hi, jnp.where(sub == 1, flat_lo, 0.0)
            ).astype(BF16)
            rhs[2 * GROUP:3 * GROUP, :] = block
            block2 = jnp.where(sub == 0, flat_hi, jnp.where(sub == 1, flat_lo, 0.0)).astype(BF16)
            sums_lhs[GROUP:2 * GROUP, :] = block2
            z = dot(lhs[g], rhs[...])
            base = base_s[...]
            for i in range(GROUP):
                at = slice(i * CP, (i + 1) * CP)
                w = z[:H, at] + base
                t = jnp.tanh(w)
                p = 1.0 + t
                y_s[:, at] = (w * p).astype(BF16)
                slope_s[:, at] = (p * (1.0 + w * (1.0 - t))).astype(slope_s.dtype)
            pm = dot(w2h, y_s[...])
            for i in range(GROUP):
                at = slice(i * CP, (i + 1) * CP)
                w = pm[:, at] + b2_b
                t = jnp.tanh(w)
                p = 1.0 + t
                e = env_s[pl.ds(first + i, 1), :]
                x3_s[L:2 * L, at] = (w * p * e).astype(BF16)
                x3_s[0:L, at] = (p * (1.0 + w * (1.0 - t)) * (z[H:, at] * e)).astype(BF16)
            gh = dot(w2t, x3_s[0:L, :])
            total = gcol[...]
            for i in range(GROUP):
                at = slice(i * CP, (i + 1) * CP)
                inner = gh[:, at] * slope_s[:, at]
                total = total + inner
                x3_s[2 * L:, at] = inner.astype(BF16)
            gcol[...] = total
            gw2[...] += dot(x3_s[0:L, :], y_s[...], NT)
            s = dot(sums_lhs[...], x3_s[...], NT)
            racc[u, pl.ds(first, GROUP), :] += s[:GROUP]
            gds[...] += s[GROUP:GROUP + 8]
            return carry

        lax.fori_loop(0, CP // GROUP, group, 0)
        cacc[v] += gcol[...]
        return carry

    lax.fori_loop(0, count_ref[0], tile, 0)

    w1rt = jnp.transpose(w1r.astype(F32)).astype(BF16)
    w1ct = jnp.transpose(w1c.astype(F32)).astype(BF16)

    def finish_row(c, carry):
        first, bias1, bias2 = carry
        acc = racc[c]
        out = lax.rem(c // CELLS - me_col + ring, ring) * CELLS + c % CELLS
        rows_ref[out, 0:L, :] = jnp.transpose(acc[:, L:2 * L]).astype(rows_ref.dtype)
        grads = acc[:, 2 * L:]
        rows_ref[out, L:2 * L, :] = dot_split(w1rt, grads, NT).astype(rows_ref.dtype)
        first = first + dot_split(r_ref[c, 0:L, :], grads)
        bias1 = bias1 + jnp.sum(grads, axis=0, keepdims=True)
        bias2 = bias2 + jnp.sum(acc[:, :2 * L], axis=0, keepdims=True)
        return first, bias1, bias2

    first_r, bias1, bias2 = lax.fori_loop(
        0, n_row, finish_row,
        (jnp.zeros((L, H), F32), jnp.zeros((1, H), F32), jnp.zeros((1, 2 * L), F32)),
    )

    def finish_col(c, first):
        grads = cacc[c]
        value = dot_split(w1ct, grads)
        slot, inner = c // CELLS, c % CELLS

        @pl.when(slot % 2 == 0)
        def _():
            colb_ref[(slot // 2) * CELLS + inner] = value

        @pl.when(slot % 2 == 1)
        def _():
            cola_ref[(slot // 2) * CELLS + inner] = value.astype(cola_ref.dtype)

        return first + dot_split(c_ref[c, 0:L, :], grads, NT)

    first_c = lax.fori_loop(0, n_col, finish_col, jnp.zeros((L, H), F32))
    par_ref[0:L, :] = first_r
    par_ref[L:2 * L, :] = first_c
    par_ref[2 * L:3 * L, :] = gw2[...]
    par_ref[3 * L:3 * L + 8, :] = jnp.zeros((8, H), F32)
    par_ref[3 * L:3 * L + 1, :] = bias1
    par_ref[3 * L + 1:3 * L + 2, :] = gds[0:1, 2 * L:] + gds[1:2, 2 * L:]
    par_ref[3 * L + 2:3 * L + 3, :] = bias2


def pair_call(count, pairs, rp, cp, w1, b1, ds, w2, b2):
    n_row, n_col = rp.shape[0], cp.shape[0]
    vm = pl.BlockSpec(memory_space=pltpu.VMEM)
    sm = pl.BlockSpec(memory_space=pltpu.SMEM)
    b2p = jnp.pad(b2, (0, 2 * L - b2.shape[0]))
    return pl.pallas_call(
        pair_kernel,
        out_shape=(
            jax.ShapeDtypeStruct((n_row, 2 * L, CP), BF16),
            jax.ShapeDtypeStruct((n_col // 2, L, CP), BF16),
            jax.ShapeDtypeStruct((n_col // 2, L, CP), F32),
            jax.ShapeDtypeStruct((3 * L + 8, H), F32),
        ),
        in_specs=[sm, sm] + [vm] * 7,
        out_specs=(vm, vm, vm, vm),
        scratch_shapes=[
            pltpu.VMEM((CP // GROUP, H + L, 64), BF16),
            pltpu.VMEM((4 * GROUP, WIDE), BF16),
            pltpu.VMEM((2 * GROUP, WIDE), BF16),
            pltpu.VMEM((CP, CP), F32),
            pltpu.VMEM((CP, CP), F32),
            pltpu.VMEM((H, CP), F32),
            pltpu.VMEM((H, WIDE), BF16),
            pltpu.VMEM((H, WIDE), F32),
            pltpu.VMEM((2 * H, WIDE), BF16),
            pltpu.VMEM((n_row, CP, 2 * H), F32),
            pltpu.VMEM((n_col, H, CP), F32),
            pltpu.VMEM((H, CP), F32),
            pltpu.VMEM((L, H), F32),
            pltpu.VMEM((8, 2 * H), F32),
        ],
        compiler_params=pltpu.CompilerParams(vmem_limit_bytes=32 * 1024 * 1024),
        name="pair_tiles",
    )(count, pairs, rp, cp, w1, b1.reshape(1, H), ds.reshape(1, H), w2, b2p.reshape(1, 2 * L))


def stepped(n, d):
    return [(i, (i + 2 * d) % n) for i in range(n)]


def per_device(
    feats, coords, valid, pairs, pair_count, w_first, bias_first, dist_scale,
    w_second, bias_second, cotangent, rows_n, cols_n,
):
    swap = [(i, i ^ 1) for i in range(rows_n)]
    halves = rows_n // 2
    extra = jnp.concatenate(
        [coords, valid.astype(BF16)[:, None], jnp.zeros((CELLS, 12, CP), BF16)], axis=1
    )
    col_own = jnp.concatenate([feats, extra], axis=1)
    row_own = jnp.concatenate([feats, cotangent, extra], axis=1)
    col_pair = jnp.concatenate([col_own, lax.ppermute(col_own, "row", swap)], axis=0)
    col_parts = [col_pair] + [
        lax.ppermute(col_pair, "row", stepped(rows_n, -d)) for d in range(1, halves)
    ]
    row_pack = lax.all_gather(row_own, "col", axis=0, tiled=True)
    col_pack = jnp.concatenate(col_parts, axis=0)
    rows_out, cola, colb, par = pair_call(
        pair_count[0], pairs[0, 0], row_pack, col_pack,
        w_first, bias_first, dist_scale, w_second, bias_second,
    )
    got_rows = [rows_out[:CELLS].astype(F32)]
    for d in range(1, cols_n):
        move = [(i, (i + d) % cols_n) for i in range(cols_n)]
        got_rows.append(
            lax.ppermute(rows_out[d * CELLS:(d + 1) * CELLS], "col", move).astype(F32)
        )
    own_rows = sum(got_rows)
    cola = lax.ppermute(cola, "row", swap)
    par = par + lax.ppermute(par, "row", swap)
    col_half = colb + cola.astype(F32)
    col_send = col_half.astype(BF16)
    own_cols = col_half[:CELLS]
    total = par
    for d in range(1, halves):
        own_cols = own_cols + lax.ppermute(
            col_send[d * CELLS:(d + 1) * CELLS], "row", stepped(rows_n, d)
        ).astype(F32)
        total = total + lax.ppermute(par, "row", stepped(rows_n, d))
    par = total
    for d in range(1, cols_n):
        move = [(i, (i + d) % cols_n) for i in range(cols_n)]
        total = total + lax.ppermute(par, "col", move)
    updated = (feats.astype(F32) + own_rows[:, :L]).astype(BF16)
    grad_feats = cotangent.astype(F32) + own_rows[:, L:] + own_cols
    return (
        updated,
        grad_feats,
        jnp.transpose(total[:2 * L]),
        total[3 * L],
        total[3 * L + 1],
        total[2 * L:3 * L],
        total[3 * L + 2, :L],
    )


def solution(mesh):
    spread = P(("row", "col"))
    placed = (spread, spread, spread, P("row", "col"), P("row", "col"), P(), P(), P(), P(), P(), spread)
    return jax.shard_map(
        functools.partial(per_device, rows_n=mesh.shape["row"], cols_n=mesh.shape["col"]),
        mesh=mesh,
        in_specs=placed,
        out_specs=(spread, spread, P(), P(), P(), P(), P()),
        check_vma=False,
    )
```

```python
import functools
import jax
import jax.numpy as jnp
from jax import lax
from jax.experimental import pallas as pl
from jax.experimental.pallas import tpu as pltpu
from jax.sharding import PartitionSpec as P

L = 64
H = 128
CP = 128
GROUP = 16
WIDE = GROUP * CP
CELLS = 2
DEEP = 4
PAR = 224
HALF = PAR // 2
NT = (((1,), (1,)), ((), ()))
NN = (((1,), (0,)), ((), ()))
F32 = jnp.float32
BF16 = jnp.bfloat16


def dot(a, b, dims=NN):
    return lax.dot_general(a, b, dims, preferred_element_type=F32)


def split(value):
    high = value.astype(BF16)
    return high, (value - high.astype(F32)).astype(BF16)


def put_split(ref, at, value):
    rows = value.shape[0]
    high, low = split(value)
    ref[at:at + rows, :] = high
    ref[at + rows:at + 2 * rows, :] = low


def get_split(ref, at, rows):
    return ref[at:at + rows, :].astype(F32) + ref[at + rows:at + 2 * rows, :].astype(F32)


def column(row, rows):
    return jnp.transpose(jnp.broadcast_to(row, (rows, row.shape[1])))


def pair_kernel(chips, steps, *refs):
    (own_ref, oth_ref), refs = refs[:2], refs[2:]
    row_refs, refs = refs[:2 * chips], refs[2 * chips:]
    col_refs, refs = refs[:2 * steps], refs[2 * steps:]
    (
        w1_ref, b1_ref, ds_ref, w2_ref, b2_ref,
        send_ref, keep_rows, keep_cols, keep_par,
        fixed, even, odd, pos, feat_b, rhs, y_s, slope_s, pm_s, x3_s, env_s, cot_s, split_s,
        racc, cacc, gw2, gds, r_ref, c_ref, par_ref,
    ) = refs
    me_row, me_col = lax.axis_index("row"), lax.axis_index("col")
    me_core = lax.rem(me_col, 2)
    half_rows = chips * CELLS
    half_cols = steps * 2 * CELLS
    for n, ref in enumerate(row_refs):
        r_ref[n * CELLS:(n + 1) * CELLS] = ref[...]
    for n, ref in enumerate(col_refs):
        c_ref[n * 2 * CELLS:(n + 1) * 2 * CELLS] = ref[...]
    slots = (own_ref.shape[0] - 1) // 2
    own_count, oth_count = own_ref[2 * slots], oth_ref[2 * slots]
    both_count = own_count + oth_count
    first_count = jnp.where(me_core == 0, own_count, oth_count)

    def place_row(cell):
        source, inner = cell // CELLS, lax.rem(cell, CELLS)
        step = lax.rem(source // 2 - me_col // 2 + chips, chips)
        return lax.rem(source + me_core, 2) * half_rows + step * CELLS + inner

    def place_col(cell):
        source, inner = cell // CELLS, lax.rem(cell, CELLS)
        step = lax.rem(source // 2 - me_row // 2 + steps, steps)
        return (step * 2 + lax.rem(source + me_row, 2)) * CELLS + inner

    def find(index):
        second = (index >= first_count).astype(jnp.int32)
        entry = index - second * first_count
        mine = second == me_core
        u = jnp.where(mine, own_ref[2 * entry], oth_ref[2 * entry])
        v = jnp.where(mine, own_ref[2 * entry + 1], oth_ref[2 * entry + 1])
        return place_row(u), place_col(v) + jnp.where(mine, 0, half_cols)

    lane = lax.broadcasted_iota(jnp.int32, (H, CP), 1)
    sub = lax.broadcasted_iota(jnp.int32, (8, CP), 0)
    lane2 = lax.broadcasted_iota(jnp.int32, (2 * H, CP), 1)
    zero8 = jnp.zeros((8, CP), F32)
    hot = (
        lax.broadcasted_iota(jnp.int32, (GROUP, WIDE), 1) // CP
        == lax.broadcasted_iota(jnp.int32, (GROUP, WIDE), 0)
    ).astype(F32).astype(BF16)
    for k in range(DEEP):
        rhs[k, 0:GROUP, :] = hot
        rhs[k, GROUP:2 * GROUP, :] = hot
        rhs[k, 2 * GROUP:3 * GROUP, :] = jnp.zeros((GROUP, WIDE), BF16)
    for k in (DEEP - 2, DEEP - 1):
        y_s[k] = jnp.zeros((H, WIDE), BF16)
    x3_s[DEEP - 2] = jnp.zeros((2 * H, WIDE), BF16)
    slope_s[DEEP - 1] = jnp.zeros((H, WIDE), BF16)
    pm_s[DEEP - 1] = jnp.zeros((L, WIDE), F32)
    env_s[DEEP - 1] = jnp.zeros((GROUP, CP), F32)
    cot_s[DEEP - 1] = jnp.zeros((L, CP), F32)
    racc[...] = jnp.zeros_like(racc)
    cacc[...] = jnp.zeros_like(cacc)
    gw2[...] = jnp.zeros_like(gw2)
    gds[...] = jnp.zeros_like(gds)
    b1_b = column(b1_ref[...], CP)
    ds_b = 0.5 * column(ds_ref[...], CP)
    b2_b = 0.5 * jnp.transpose(jnp.broadcast_to(b2_ref[...], (CP, 2 * L)))[:L, :]
    ds_hi = ds_b.astype(BF16).astype(F32)
    ds_lo = ds_b - ds_hi
    w1 = w1_ref[...]
    w1r = w1[:, :L]
    w1f = 0.5 * w1.astype(F32)
    w1f = pltpu.roll(w1f, L, 1)
    fixed[...] = jnp.where(
        lane < L, w1f, jnp.where(lane < 98, ds_hi, jnp.where(lane < 99, ds_lo, 0.0))
    )
    w2f = 0.5 * w2_ref[...].astype(F32)
    w2h = w2f.astype(BF16)
    w2t = jnp.transpose(w2f).astype(BF16)

    def forward_start(k, g):
        first = pl.multiple_of(g * GROUP, GROUP)
        rows = pl.ds(first, GROUP)
        sq = jnp.zeros((GROUP, CP), F32)
        for d in range(3):
            off = pos[d, rows, :] - pos[4, d:d + 1, :]
            sq = sq + off * off
        env_s[k] = pos[3, rows, :] * pos[4, 3:4, :] / ((1.0 + sq) * CP)
        sq_hi = sq.astype(BF16).astype(F32)
        split_s[k, 0:GROUP, :] = sq_hi
        split_s[k, GROUP:2 * GROUP, :] = sq - sq_hi
        for i in range(GROUP):
            at = slice(i * CP, (i + 1) * CP)
            hi_b = jnp.broadcast_to(split_s[k, i:i + 1, :], (8, CP))
            lo_b = jnp.broadcast_to(split_s[k, GROUP + i:GROUP + i + 1, :], (8, CP))
            top = jnp.where(sub == 1, lo_b, jnp.where(sub < 3, hi_b, 0.0))
            rhs[k, 2 * GROUP:3 * GROUP, at] = jnp.concatenate([top, zero8], axis=0).astype(BF16)
        part = pltpu.roll((even if k % 2 == 0 else odd)[...], lax.rem(L - first + CP, CP), 1)
        mix = jnp.where((lane >= L) & (lane < 96), part, fixed[...]).astype(BF16)
        cot_s[k] = pltpu.roll(cot_s[DEEP], lax.rem(CP - first, CP), 1)
        return dot(mix[:, :112], jnp.concatenate([feat_b[...], rhs[k]], axis=0))

    def forward_hidden(k, z):
        for i in range(GROUP):
            at = slice(i * CP, (i + 1) * CP)
            w = z[:, at]
            p = 1.0 + jnp.tanh(w)
            y = (w * p).astype(BF16)
            y_s[k, :, at] = y
            p = p.astype(BF16)
            slope_s[k, :, at] = p + y * (2.0 - p)
        pm_s[k] = dot(w2h, y_s[k])

    def back_message(k):
        for i in range(GROUP):
            at = slice(i * CP, (i + 1) * CP)
            w = pm_s[k, :, at] + b2_b
            t = jnp.tanh(w)
            p = 1.0 + t
            y = w * p
            e = env_s[k, i:i + 1, :]
            x3_s[k, L:2 * L, at] = (y * e).astype(BF16)
            x3_s[k, 0:L, at] = ((p + y - y * t) * (cot_s[k, :, i:i + 1] * e)).astype(BF16)
        return dot(w2t, x3_s[k, 0:L, :])

    def back_hidden(k, gh, v):
        total = cacc[v]
        for i in range(GROUP):
            at = slice(i * CP, (i + 1) * CP)
            inner = gh[:, at].astype(BF16) * slope_s[k, :, at]
            x3_s[k, 2 * L:, at] = inner
            total = total + inner.astype(F32)
        cacc[v] = total

    def back_sums(k, g, u):
        first = pl.multiple_of(g * GROUP, GROUP)
        both = jnp.concatenate([y_s[k], rhs[k, GROUP:3 * GROUP]], axis=0)
        s = dot(x3_s[k], both, NT)
        gw2[...] += s[:L, :H]
        sums = jnp.concatenate([s[:, H:], jnp.zeros((2 * H, CP - 2 * GROUP), F32)], axis=1)
        gds[...] += sums[2 * L:]
        here = (lane2 >= first) & (lane2 < first + GROUP)
        racc[u] += jnp.where(here, pltpu.roll(sums, first, 1), 0.0)

    def half(k, g, v, g_sums, u_sums):
        back = (k - 1) % DEEP
        z = forward_start(k, g)
        back_sums((k - 2) % DEEP, g_sums, u_sums)
        gh = back_message(back)
        forward_hidden(k, z)
        back_hidden(back, gh, v)

    def begin(u, v):
        a = 0.5 * (dot(w1r, r_ref[u, 0:L, :]) + b1_b)
        a_hi = a.astype(BF16).astype(F32)
        a_lo = pltpu.roll(a - a_hi, GROUP, 1)
        block = (lane // GROUP) % 2 == 0
        even[...] = jnp.where(block, a_hi, a_lo)
        odd[...] = jnp.where(block, a_lo, a_hi)
        cot_s[DEEP] = 0.5 * r_ref[u, L:2 * L, :].astype(F32)
        xu = r_ref[u, 2 * L:2 * L + 16, :].astype(F32)
        for d in range(4):
            pos[d] = column(xu[d:d + 1, :], CP)
        pos[4, 0:16, :] = c_ref[v, L:L + 16, :].astype(F32)
        fv = c_ref[v, 0:L, :]
        for i in range(GROUP):
            feat_b[:, i * CP:(i + 1) * CP] = fv

    parts = CP // GROUP // DEEP
    begins = jnp.where(me_core == 0, 0, both_count * parts // 2)
    ends = jnp.where(me_core == 0, both_count * parts // 2, both_count * parts)

    def unit(index, before):
        u_last, v_last, g_last = before
        u, v = find(index // parts)
        g = lax.rem(index, parts) * DEEP

        @pl.when((g == 0) | (index == begins))
        def _():
            begin(u, v)

        for k in range(DEEP):
            g_sums = g + k - 2 if k >= 2 else g_last + DEEP + k - 2
            half(k, g + k, v if k else v_last, g_sums, u if k >= 2 else u_last)
        return u, v, g

    zero = jnp.int32(0)
    u, v, g = lax.fori_loop(begins, ends, unit, (zero, zero, zero))
    gh = back_message(DEEP - 1)
    back_sums(DEEP - 2, g + DEEP - 2, u)
    back_hidden(DEEP - 1, gh, v)
    back_sums(DEEP - 1, g + DEEP - 1, u)

    w1t = 2.0 * jnp.transpose(w1f)
    ones = jnp.ones((GROUP, 8 * CP), BF16)
    par_ref[2 * L:3 * L, :] = gw2[...]
    par_ref[3 * L:, :] = jnp.zeros((PAR - 3 * L, H), F32)
    picked = ((lane >= GROUP) & (lane < GROUP + 2))[:GROUP].astype(F32).astype(BF16)
    high, low = split(gds[...])
    par_ref[3 * L + 1:3 * L + 2, :] = (dot(picked, high, NT) + dot(picked, low, NT))[0:1]

    def block(acc, src, w, start, count, put):
        cells = [start + n for n in range(count)]
        grads = jnp.concatenate([acc[c, acc.shape[1] - H:, :] for c in cells], axis=1)
        feats = jnp.concatenate([src[c, 0:L, :] for c in cells], axis=1)
        high, low = split(grads)
        values = dot(w, high) + dot(w, low)
        left = jnp.concatenate([feats, ones[:, :count * CP]], axis=0)
        for n, c in enumerate(cells):
            put(c, values[:, n * CP:(n + 1) * CP])
        return dot(left, high, NT) + dot(left, low, NT)

    def keep_row(c, value):
        keep_rows[c, 0:L, :] = racc[c, L:2 * L, :]
        keep_rows[c, L:2 * L, :] = value

    def send_row(c, value):
        at = pl.multiple_of((c - half_rows) * 2 * L, 2 * L)
        send_ref[pl.ds(at, L), :] = racc[c, L:2 * L, :].astype(BF16)
        send_ref[pl.ds(at + L, L), :] = value.astype(BF16)

    def keep_col(c, value):
        keep_cols[c] = value

    def send_col(c, value):
        at = pl.multiple_of(half_rows * 2 * L + (c - half_cols) * L, L)
        send_ref[pl.ds(at, L), :] = value.astype(BF16)

    def sweep(acc, src, w, start, total, count, put):
        return lax.fori_loop(
            0, total // count,
            lambda n, part: part + block(acc, src, w, start + n * count, count, put),
            jnp.zeros((L + GROUP, H), F32),
        )

    w_row, w_col = w1t[L:].astype(BF16), w1t[:L].astype(BF16)
    first = sweep(racc, r_ref, w_row, 0, half_rows, 4, keep_row)
    first = first + sweep(racc, r_ref, w_row, half_rows, half_rows, 4, send_row)
    par_ref[0:L, :] = first[:L]
    par_ref[3 * L:3 * L + 1, :] = first[L:L + 1]
    bias2 = jnp.zeros((2 * L, CP), F32)
    for c in range(2 * half_rows):
        bias2 = bias2 + racc[c, :2 * L, :]
    high, low = split(bias2)
    one = ones[:, :CP]
    par_ref[3 * L + 2:3 * L + 3, :] = (dot(one, high, NT) + dot(one, low, NT))[0:1]
    first = sweep(cacc, c_ref, w_col, 0, half_cols, 8, keep_col)
    first = first + sweep(cacc, c_ref, w_col, half_cols, half_cols, 8, send_col)
    par_ref[L:2 * L, :] = first[:L]
    keep_par[...] = par_ref[pl.ds(pl.multiple_of(me_core * HALF, HALF), HALF), :]
    put_split(send_ref, half_rows * 2 * L + half_cols * L,
              par_ref[pl.ds(pl.multiple_of((1 - me_core) * HALF, HALF), HALF), :])


VM = pl.BlockSpec(memory_space=pltpu.VMEM)
SM = pl.BlockSpec(memory_space=pltpu.SMEM)


def call(kernel, name, ins, outs, scratch=(), smem=0, limit=48):
    return pl.pallas_call(
        kernel,
        out_shape=tuple(jax.ShapeDtypeStruct(s, d) for s, d in outs),
        in_specs=[SM] * smem + [VM] * (len(ins) - smem),
        out_specs=(VM,) * len(outs),
        scratch_shapes=list(scratch),
        compiler_params=pltpu.CompilerParams(vmem_limit_bytes=limit * 1024 * 1024),
        name=name,
    )(*ins)


def pair_call(lists, rows, cols, weights):
    chips, steps = len(rows) // 2, len(cols) // 2
    n_row, n_col = 2 * chips * CELLS, 4 * steps * CELLS
    sent = n_row // 2 * 2 * L + n_col // 2 * L + PAR
    return call(
        functools.partial(pair_kernel, chips, steps),
        "pair_tiles",
        [*lists, *rows, *cols, *weights],
        [
            ((sent, CP), BF16),
            ((n_row // 2, 2 * L, CP), F32),
            ((n_col // 2, L, CP), F32),
            ((HALF, H), F32),
        ],
        [
            pltpu.VMEM((H, CP), F32),
            pltpu.VMEM((H, CP), F32),
            pltpu.VMEM((H, CP), F32),
            pltpu.VMEM((5, CP, CP), F32),
            pltpu.VMEM((L, WIDE), BF16),
            pltpu.VMEM((DEEP, 3 * GROUP, WIDE), BF16),
            pltpu.VMEM((DEEP, H, WIDE), BF16),
            pltpu.VMEM((DEEP, H, WIDE), BF16),
            pltpu.VMEM((DEEP, L, WIDE), F32),
            pltpu.VMEM((DEEP, 2 * H, WIDE), BF16),
            pltpu.VMEM((DEEP, GROUP, CP), F32),
            pltpu.VMEM((DEEP + 1, L, CP), F32),
            pltpu.VMEM((DEEP, 2 * GROUP, CP), F32),
            pltpu.VMEM((n_row, 2 * H, CP), F32),
            pltpu.VMEM((n_col, H, CP), F32),
            pltpu.VMEM((L, H), F32),
            pltpu.VMEM((H, CP), F32),
            pltpu.VMEM((n_row,) + rows[0].shape[1:], BF16),
            pltpu.VMEM((n_col,) + cols[0].shape[1:], BF16),
            pltpu.VMEM((PAR, H), F32),
        ],
        smem=2,
    )


def core_sum(chips, steps, recv, rows, cols, par, *outs):
    x_msgs, (y_msg, xy_msg, rows_out, cols_out, par_out) = outs[:chips - 1], outs[chips - 1:]
    n_row, n_col = rows.shape[0], cols.shape[0]
    total = par[...] + get_split(recv, n_row * 2 * L + n_col * L, HALF)
    par_out[...] = total
    put_split(xy_msg, 0, total)
    for c in range(n_row):
        value = rows[c] + recv[c * 2 * L:(c + 1) * 2 * L, :].astype(F32)
        step, inner = c // CELLS, c % CELLS
        if step == 0:
            rows_out[inner] = value
        else:
            x_msgs[step - 1][inner * 2 * L:(inner + 1) * 2 * L, :] = value.astype(BF16)
    for x_msg in x_msgs:
        put_split(x_msg, CELLS * 2 * L, total)
    for c in range(n_col):
        at = n_row * 2 * L + c * L
        value = cols[c] + recv[at:at + L, :].astype(F32)
        slot, inner = c // CELLS, c % CELLS
        to = (slot // 2) * CELLS + inner
        if slot % 2 == 0:
            cols_out[to] = value
        else:
            y_msg[to * L:(to + 1) * L, :] = value.astype(BF16)
    put_split(y_msg, steps * CELLS * L, total)


def near_sum(chips, steps, *refs):
    x_in, refs = refs[:chips - 1], refs[chips - 1:]
    xy_in, refs = refs[:chips - 1], refs[chips - 1:]
    (y_in, rows, cols, par), refs = refs[:4], refs[4:]
    rows_out, cols_out, par_out = refs[:3]
    z_msgs = refs[3:]
    total = par[...] + get_split(y_in, steps * CELLS * L, HALF)
    for ref in x_in:
        total = total + get_split(ref, CELLS * 2 * L, HALF)
    for ref in xy_in:
        total = total + get_split(ref, 0, HALF)
    par_out[...] = total
    for c in range(CELLS):
        value = rows[c]
        for ref in x_in:
            value = value + ref[c * 2 * L:(c + 1) * 2 * L, :].astype(F32)
        rows_out[c] = value
    for c in range(steps * CELLS):
        value = cols[c] + y_in[c * L:(c + 1) * L, :].astype(F32)
        step, inner = c // CELLS, c % CELLS
        if step == 0:
            cols_out[inner] = value
        else:
            z_msgs[step - 1][inner * L:(inner + 1) * L, :] = value.astype(BF16)
    for ref in z_msgs:
        put_split(ref, CELLS * L, total)


def far_sum(steps, *refs):
    z_in, refs = refs[:steps - 1], refs[steps - 1:]
    rows, cols, par, feats, cotangent, updated, grad_feats, par_out = refs
    total = par[...]
    for ref in z_in:
        total = total + get_split(ref, CELLS * L, HALF)
    par_out[...] = total
    for c in range(CELLS):
        value = cols[c]
        for ref in z_in:
            value = value + ref[c * L:(c + 1) * L, :].astype(F32)
        updated[c] = (feats[c].astype(F32) + rows[c, :L, :]).astype(BF16)
        grad_feats[c] = cotangent[c].astype(F32) + rows[c, L:, :] + value


def gather_halves(own, oth, first, bias1, dist, second, bias2, par):
    core = lax.rem(lax.axis_index("col"), 2)
    par[pl.ds(pl.multiple_of(core * HALF, HALF), HALF), :] = own[...]
    par[pl.ds(pl.multiple_of((1 - core) * HALF, HALF), HALF), :] = oth[...]
    first[...] = jnp.transpose(par[:2 * L, :])
    second[...] = par[2 * L:3 * L, :]
    bias1[...] = par[3 * L:3 * L + 1, :]
    dist[...] = par[3 * L + 1:3 * L + 2, :]
    bias2[...] = par[3 * L + 2:3 * L + 3, :]


def per_device(
    feats, coords, valid, pairs, pair_count, w_first, bias_first, dist_scale,
    w_second, bias_second, cotangent, rows_n, cols_n,
):
    steps, chips = rows_n // 2, cols_n // 2
    swap_y = [(i, i ^ 1) for i in range(rows_n)]
    swap_core = [(i, i ^ 1) for i in range(cols_n)]

    def along(n, d):
        return [(i, (i + 2 * d) % n) for i in range(n)]

    def diagonal(d):
        return [
            (r * cols_n + c, (r ^ 1) * cols_n + (c + 2 * d) % cols_n)
            for r in range(rows_n) for c in range(cols_n)
        ]

    extra = jnp.concatenate(
        [coords, valid.astype(BF16)[:, None], jnp.zeros((CELLS, 12, CP), BF16)], axis=1
    )
    col_own = jnp.concatenate([feats, extra], axis=1)
    row_own = jnp.concatenate([feats, cotangent, extra], axis=1)
    tiles = jnp.concatenate([pairs.reshape(-1), pair_count.reshape(-1)])
    col_pair = jnp.concatenate([col_own, lax.ppermute(col_own, "row", swap_y)], axis=0)
    row_parts = [row_own] + [
        lax.ppermute(row_own, "col", along(cols_n, -d)) for d in range(1, chips)
    ]
    col_parts = [col_pair] + [
        lax.ppermute(col_pair, "row", along(rows_n, -d)) for d in range(1, steps)
    ]
    other_tiles = lax.ppermute(tiles, "col", swap_core)
    row_parts += [lax.ppermute(p, "col", swap_core) for p in row_parts]
    col_parts += [lax.ppermute(p, "col", swap_core) for p in col_parts]
    send, rows, cols, par = pair_call(
        [tiles, other_tiles], row_parts, col_parts,
        [
            w_first, bias_first.reshape(1, H), dist_scale.reshape(1, H), w_second,
            jnp.pad(bias_second, (0, L)).reshape(1, 2 * L),
        ],
    )
    got = lax.ppermute(send, "col", swap_core)
    x_shape = ((CELLS * 2 * L + PAR, CP), BF16)
    keep = [((CELLS, 2 * L, CP), F32), ((steps * CELLS, L, CP), F32), ((HALF, H), F32)]
    outs = call(
        functools.partial(core_sum, chips, steps), "core_sum", [got, rows, cols, par],
        [x_shape] * (chips - 1)
        + [((steps * CELLS * L + PAR, CP), BF16), ((PAR, H), BF16)] + keep,
    )
    x_msgs, (y_msg, xy_msg, rows, cols, par) = outs[:chips - 1], outs[chips - 1:]
    y_in = lax.ppermute(y_msg, "row", swap_y)
    x_in = [lax.ppermute(m, "col", along(cols_n, d + 1)) for d, m in enumerate(x_msgs)]
    xy_in = [lax.ppermute(xy_msg, ("row", "col"), diagonal(d)) for d in range(1, chips)]
    keep[1] = ((CELLS, L, CP), F32)
    rows, cols, par, *z_msgs = call(
        functools.partial(near_sum, chips, steps), "near_sum",
        [*x_in, *xy_in, y_in, rows, cols, par],
        keep + [((CELLS * L + PAR, CP), BF16)] * (steps - 1),
    )
    z_in = [lax.ppermute(m, "row", along(rows_n, d + 1)) for d, m in enumerate(z_msgs)]
    updated, grad_feats, par = call(
        functools.partial(far_sum, steps), "far_sum",
        [*z_in, rows, cols, par, feats, cotangent],
        [((CELLS, L, CP), BF16), ((CELLS, L, CP), F32), ((HALF, H), F32)],
    )
    first, bias1, dist, second, bias2 = call(
        gather_halves, "gather_halves", [par, lax.ppermute(par, "col", swap_core)],
        [((H, 2 * L), F32), ((1, H), F32), ((1, H), F32), ((L, H), F32), ((1, H), F32)],
        [pltpu.VMEM((PAR, H), F32)],
    )
    return updated, grad_feats, first, bias1[0], dist[0], second, bias2[0, :L]


def solution(mesh):
    spread = P(("row", "col"))
    placed = (spread, spread, spread, P("row", "col"), P("row", "col"), P(), P(), P(), P(), P(), spread)
    return jax.shard_map(
        functools.partial(per_device, rows_n=mesh.shape["row"], cols_n=mesh.shape["col"]),
        mesh=mesh,
        in_specs=placed,
        out_specs=(spread, spread, P(), P(), P(), P(), P()),
        check_vma=False,
    )
```

```python
import functools
import jax
import jax.numpy as jnp
from jax import lax
from jax.experimental import pallas as pl
from jax.experimental.pallas import tpu as pltpu
from jax.sharding import PartitionSpec as P

L = 64
H = 128
CP = 128
GROUP = 16
WIDE = GROUP * CP
CELLS = 2
DEEP = 4
PAR = 224
HALF = PAR // 2
CHUNK = 8
QUAD = 4
NT = (((1,), (1,)), ((), ()))
NN = (((1,), (0,)), ((), ()))
F32 = jnp.float32
BF16 = jnp.bfloat16


def dot(a, b, dims=NN):
    return lax.dot_general(a, b, dims, preferred_element_type=F32)


def split(value):
    high = value.astype(BF16)
    return high, (value - high.astype(F32)).astype(BF16)


def put_split(ref, at, value):
    rows = value.shape[0]
    high, low = split(value)
    ref[at:at + rows, :] = high
    ref[at + rows:at + 2 * rows, :] = low


def get_split(ref, at, rows):
    return ref[at:at + rows, :].astype(F32) + ref[at + rows:at + 2 * rows, :].astype(F32)


def column(row, rows):
    return jnp.transpose(jnp.broadcast_to(row, (rows, row.shape[1])))


def pair_kernel(chips, steps, *refs):
    (own_ref, oth_ref), refs = refs[:2], refs[2:]
    row_refs, refs = refs[:2 * chips], refs[2 * chips:]
    col_refs, refs = refs[:2 * steps], refs[2 * steps:]
    (
        w1_ref, b1_ref, ds_ref, w2_ref, b2_ref,
        send_ref, keep_rows, keep_cols, keep_par,
        fixed, even, odd, pos, feat_b, rhs, y_s, slope_s, pm_s, x3_s, env_s, cot_s, split_s,
        racc, cacc, gw2, gds, r_ref, c_ref, par_ref,
    ) = refs
    me_row, me_col = lax.axis_index("row"), lax.axis_index("col")
    me_core = lax.rem(me_col, 2)
    half_rows = chips * CELLS
    half_cols = steps * 2 * CELLS
    for n, ref in enumerate(row_refs):
        r_ref[n * CELLS:(n + 1) * CELLS] = ref[...]
    for n, ref in enumerate(col_refs):
        c_ref[n * 2 * CELLS:(n + 1) * 2 * CELLS] = ref[...]
    slots = (own_ref.shape[0] - 1) // 2
    own_count, oth_count = own_ref[2 * slots], oth_ref[2 * slots]
    both_count = own_count + oth_count
    first_count = jnp.where(me_core == 0, own_count, oth_count)

    def place_row(cell):
        source, inner = cell // CELLS, lax.rem(cell, CELLS)
        step = lax.rem(source // 2 - me_col // 2 + chips, chips)
        return lax.rem(source + me_core, 2) * half_rows + step * CELLS + inner

    def place_col(cell):
        source, inner = cell // CELLS, lax.rem(cell, CELLS)
        step = lax.rem(source // 2 - me_row // 2 + steps, steps)
        return (step * 2 + lax.rem(source + me_row, 2)) * CELLS + inner

    def find(index):
        second = (index >= first_count).astype(jnp.int32)
        entry = index - second * first_count
        mine = second == me_core
        u = jnp.where(mine, own_ref[2 * entry], oth_ref[2 * entry])
        v = jnp.where(mine, own_ref[2 * entry + 1], oth_ref[2 * entry + 1])
        return place_row(u), place_col(v) + jnp.where(mine, 0, half_cols)

    lane = lax.broadcasted_iota(jnp.int32, (H, CP), 1)
    sub = lax.broadcasted_iota(jnp.int32, (8, CP), 0)
    lane2 = lax.broadcasted_iota(jnp.int32, (2 * H, CP), 1)
    zero8 = jnp.zeros((8, CP), F32)
    hot = (
        lax.broadcasted_iota(jnp.int32, (GROUP, WIDE), 1) // CP
        == lax.broadcasted_iota(jnp.int32, (GROUP, WIDE), 0)
    ).astype(F32).astype(BF16)
    for k in range(DEEP):
        rhs[k, 0:GROUP, :] = hot
        rhs[k, GROUP:2 * GROUP, :] = hot
        rhs[k, 2 * GROUP:3 * GROUP, :] = jnp.zeros((GROUP, WIDE), BF16)
    for k in (DEEP - 2, DEEP - 1):
        y_s[k] = jnp.zeros((H, WIDE), BF16)
    x3_s[DEEP - 2] = jnp.zeros((2 * H, WIDE), BF16)
    slope_s[DEEP - 1] = jnp.zeros((H, WIDE), BF16)
    pm_s[DEEP - 1] = jnp.zeros((L, WIDE), F32)
    env_s[DEEP - 1] = jnp.zeros((GROUP, CP), F32)
    cot_s[DEEP - 1] = jnp.zeros((L, CP), F32)
    racc[...] = jnp.zeros_like(racc)
    cacc[...] = jnp.zeros_like(cacc)
    gw2[...] = jnp.zeros_like(gw2)
    gds[...] = jnp.zeros_like(gds)
    b1_b = column(b1_ref[...], CP)
    ds_b = 0.5 * column(ds_ref[...], CP)
    b2_b = 0.5 * jnp.transpose(jnp.broadcast_to(b2_ref[...], (CP, 2 * L)))[:L, :]
    ds_hi = ds_b.astype(BF16).astype(F32)
    ds_lo = ds_b - ds_hi
    w1 = w1_ref[...]
    w1r = w1[:, :L]
    w1f = 0.5 * w1.astype(F32)
    w1f = pltpu.roll(w1f, L, 1)
    fixed[...] = jnp.where(
        lane < L, w1f, jnp.where(lane < 98, ds_hi, jnp.where(lane < 99, ds_lo, 0.0))
    )
    w2f = 0.5 * w2_ref[...].astype(F32)
    w2h = w2f.astype(BF16)
    w2t = jnp.transpose(w2f).astype(BF16)

    def forward_start(k, g):
        first = pl.multiple_of(g * GROUP, GROUP)
        rows = pl.ds(first, GROUP)
        sq = jnp.zeros((GROUP, CP), F32)
        for d in range(3):
            off = pos[d, rows, :] - pos[4, d:d + 1, :]
            sq = sq + off * off
        env_s[k] = pos[3, rows, :] * pos[4, 3:4, :] / ((1.0 + sq) * CP)
        sq_hi = sq.astype(BF16).astype(F32)
        split_s[k, 0:GROUP, :] = sq_hi
        split_s[k, GROUP:2 * GROUP, :] = sq - sq_hi
        for i in range(GROUP):
            at = slice(i * CP, (i + 1) * CP)
            hi_b = jnp.broadcast_to(split_s[k, i:i + 1, :], (8, CP))
            lo_b = jnp.broadcast_to(split_s[k, GROUP + i:GROUP + i + 1, :], (8, CP))
            top = jnp.where(sub == 1, lo_b, jnp.where(sub < 3, hi_b, 0.0))
            rhs[k, 2 * GROUP:3 * GROUP, at] = jnp.concatenate([top, zero8], axis=0).astype(BF16)
        part = pltpu.roll((even if k % 2 == 0 else odd)[...], lax.rem(L - first + CP, CP), 1)
        mix = jnp.where((lane >= L) & (lane < 96), part, fixed[...]).astype(BF16)
        cot_s[k] = pltpu.roll(cot_s[DEEP], lax.rem(CP - first, CP), 1)
        return mix[:, :112]

    def lanes(c):
        return slice(c * CHUNK * CP, (c + 1) * CHUNK * CP)

    def first_layer(k, mix, c):
        return dot(mix, jnp.concatenate([feat_b[:, lanes(c)], rhs[k, :, lanes(c)]], axis=0))

    def forward_hidden(k, z, c):
        for i in range(CHUNK):
            at = slice((c * CHUNK + i) * CP, (c * CHUNK + i + 1) * CP)
            w = z[:, i * CP:(i + 1) * CP]
            p = 1.0 + jnp.tanh(w)
            y = (w * p).astype(BF16)
            y_s[k, :, at] = y
            p = p.astype(BF16)
            slope_s[k, :, at] = p + y * (2.0 - p)
        pm_s[k, :, lanes(c)] = dot(w2h, y_s[k, :, lanes(c)])

    def back_message(k, c):
        for i in range(c * CHUNK, (c + 1) * CHUNK):
            at = slice(i * CP, (i + 1) * CP)
            w = pm_s[k, :, at] + b2_b
            t = jnp.tanh(w)
            p = 1.0 + t
            y = w * p
            e = env_s[k, i:i + 1, :]
            x3_s[k, L:2 * L, at] = (y * e).astype(BF16)
            x3_s[k, 0:L, at] = ((p + y - y * t) * (cot_s[k, :, i:i + 1] * e)).astype(BF16)
        return dot(w2t, x3_s[k, 0:L, lanes(c)])

    def back_hidden(k, gh, total, c):
        for q in range(0, CHUNK, QUAD):
            some = None
            for i in range(q, q + QUAD):
                at = slice((c * CHUNK + i) * CP, (c * CHUNK + i + 1) * CP)
                inner = gh[:, i * CP:(i + 1) * CP].astype(BF16) * slope_s[k, :, at]
                x3_s[k, 2 * L:, at] = inner
                some = inner if some is None else some + inner
            total = total + some.astype(F32)
        return total

    def sums(k):
        both = jnp.concatenate([y_s[k], rhs[k, GROUP:3 * GROUP]], axis=0)
        return dot(both, jnp.transpose(x3_s[k]))

    def put_sums(s, g, u):
        first = pl.multiple_of(g * GROUP, GROUP)
        gw2[...] += s[:H, :H]
        racc[u, pl.ds(first, GROUP), :] += s[H:H + GROUP]
        gds[0:8] += s[H + GROUP:H + GROUP + 8]

    def half(k, g, v, g_sums, u_sums):
        back = (k - 1) % DEEP
        old = (k - 2) % DEEP
        chunks = GROUP // CHUNK
        mix = forward_start(k, g)
        total = cacc[v]
        s = None
        late = None
        s = sums(old)
        for c in range(chunks):
            z = first_layer(k, mix, c)
            gh = back_message(back, c)
            forward_hidden(k, z, c)
            total = back_hidden(back, gh, total, c)
        cacc[v] = total
        put_sums(s, g_sums, u_sums)

    def begin(u, v):
        a = 0.5 * (dot(w1r, r_ref[u, 0:L, :]) + b1_b)
        a_hi = a.astype(BF16).astype(F32)
        a_lo = pltpu.roll(a - a_hi, GROUP, 1)
        block = (lane // GROUP) % 2 == 0
        even[...] = jnp.where(block, a_hi, a_lo)
        odd[...] = jnp.where(block, a_lo, a_hi)
        cot_s[DEEP] = 0.5 * r_ref[u, L:2 * L, :].astype(F32)
        xu = r_ref[u, 2 * L:2 * L + 16, :].astype(F32)
        for d in range(4):
            pos[d] = column(xu[d:d + 1, :], CP)
        pos[4, 0:16, :] = c_ref[v, L:L + 16, :].astype(F32)
        fv = c_ref[v, 0:L, :]
        for i in range(GROUP):
            feat_b[:, i * CP:(i + 1) * CP] = fv

    parts = CP // GROUP // DEEP
    begins = jnp.where(me_core == 0, 0, both_count * parts // 2)
    ends = jnp.where(me_core == 0, both_count * parts // 2, both_count * parts)

    def unit(index, before):
        u_last, v_last, g_last = before
        u, v = find(index // parts)
        g = lax.rem(index, parts) * DEEP

        @pl.when((g == 0) | (index == begins))
        def _():
            begin(u, v)

        for k in range(DEEP):
            g_sums = g + k - 2 if k >= 2 else g_last + DEEP + k - 2
            half(k, g + k, v if k else v_last, g_sums, u if k >= 2 else u_last)
        return u, v, g

    zero = jnp.int32(0)
    u, v, g = lax.fori_loop(begins, ends, unit, (zero, zero, zero))
    total = cacc[v]
    for c in range(GROUP // CHUNK):
        total = back_hidden(DEEP - 1, back_message(DEEP - 1, c), total, c)
    cacc[v] = total
    put_sums(sums(DEEP - 2), g + DEEP - 2, u)
    put_sums(sums(DEEP - 1), g + DEEP - 1, u)

    w1t = 2.0 * jnp.transpose(w1f)
    ones = jnp.ones((GROUP, 8 * CP), BF16)
    par_ref[2 * L:3 * L, :] = jnp.transpose(gw2[...])[:L]
    par_ref[3 * L:, :] = jnp.zeros((PAR - 3 * L, H), F32)
    par_ref[3 * L + 1:3 * L + 2, :] = gds[0:1, H:] + gds[1:2, H:]

    def left_of(src, cells):
        feats = jnp.concatenate([src[c, 0:L, :] for c in cells], axis=1)
        return jnp.concatenate([feats, ones[:, :len(cells) * CP]], axis=0)

    def row_block(start, count, put):
        cells = [start + n for n in range(count)]
        high, low = split(jnp.concatenate([racc[c, :, H:] for c in cells], axis=0))
        values = dot(w_row, high, NT) + dot(w_row, low, NT)
        for n, c in enumerate(cells):
            put(c, values[:, n * CP:(n + 1) * CP], jnp.transpose(racc[c, :, :H])[L:])
        left = left_of(r_ref, cells)
        return dot(left, high) + dot(left, low)

    def col_block(start, count, put):
        cells = [start + n for n in range(count)]
        high, low = split(jnp.concatenate([cacc[c] for c in cells], axis=1))
        values = dot(w_col, high) + dot(w_col, low)
        for n, c in enumerate(cells):
            put(c, values[:, n * CP:(n + 1) * CP])
        left = left_of(c_ref, cells)
        return dot(left, high, NT) + dot(left, low, NT)

    def keep_row(c, value, message):
        keep_rows[c, 0:L, :] = message
        keep_rows[c, L:2 * L, :] = value

    def send_row(c, value, message):
        at = pl.multiple_of((c - half_rows) * 2 * L, 2 * L)
        send_ref[pl.ds(at, L), :] = message.astype(BF16)
        send_ref[pl.ds(at + L, L), :] = value.astype(BF16)

    def keep_col(c, value):
        keep_cols[c] = value

    def send_col(c, value):
        at = pl.multiple_of(half_rows * 2 * L + (c - half_cols) * L, L)
        send_ref[pl.ds(at, L), :] = value.astype(BF16)

    def sweep(block, start, total, count, put):
        return lax.fori_loop(
            0, total // count,
            lambda n, part: part + block(start + n * count, count, put),
            jnp.zeros((L + GROUP, H), F32),
        )

    w_row, w_col = w1t[L:].astype(BF16), w1t[:L].astype(BF16)
    first = sweep(row_block, 0, half_rows, 4, keep_row)
    first = first + sweep(row_block, half_rows, half_rows, 4, send_row)
    par_ref[0:L, :] = first[:L]
    par_ref[3 * L:3 * L + 1, :] = first[L:L + 1]
    bias2 = jnp.zeros((1, H), F32)
    for c in range(2 * half_rows):
        bias2 = bias2 + jnp.sum(racc[c, :, :H], axis=0, keepdims=True)
    par_ref[3 * L + 2:3 * L + 3, :] = bias2
    first = sweep(col_block, 0, half_cols, 8, keep_col)
    first = first + sweep(col_block, half_cols, half_cols, 8, send_col)
    par_ref[L:2 * L, :] = first[:L]
    keep_par[...] = par_ref[pl.ds(pl.multiple_of(me_core * HALF, HALF), HALF), :]
    put_split(send_ref, half_rows * 2 * L + half_cols * L,
              par_ref[pl.ds(pl.multiple_of((1 - me_core) * HALF, HALF), HALF), :])


VM = pl.BlockSpec(memory_space=pltpu.VMEM)
SM = pl.BlockSpec(memory_space=pltpu.SMEM)


def call(kernel, name, ins, outs, scratch=(), smem=0, limit=48):
    return pl.pallas_call(
        kernel,
        out_shape=tuple(jax.ShapeDtypeStruct(s, d) for s, d in outs),
        in_specs=[SM] * smem + [VM] * (len(ins) - smem),
        out_specs=(VM,) * len(outs),
        scratch_shapes=list(scratch),
        compiler_params=pltpu.CompilerParams(vmem_limit_bytes=limit * 1024 * 1024),
        name=name,
    )(*ins)


def pair_call(lists, rows, cols, weights):
    chips, steps = len(rows) // 2, len(cols) // 2
    n_row, n_col = 2 * chips * CELLS, 4 * steps * CELLS
    sent = n_row // 2 * 2 * L + n_col // 2 * L + PAR
    return call(
        functools.partial(pair_kernel, chips, steps),
        "pair_tiles",
        [*lists, *rows, *cols, *weights],
        [
            ((sent, CP), BF16),
            ((n_row // 2, 2 * L, CP), F32),
            ((n_col // 2, L, CP), F32),
            ((HALF, H), F32),
        ],
        [
            pltpu.VMEM((H, CP), F32),
            pltpu.VMEM((H, CP), F32),
            pltpu.VMEM((H, CP), F32),
            pltpu.VMEM((5, CP, CP), F32),
            pltpu.VMEM((L, WIDE), BF16),
            pltpu.VMEM((DEEP, 3 * GROUP, WIDE), BF16),
            pltpu.VMEM((DEEP, H, WIDE), BF16),
            pltpu.VMEM((DEEP, H, WIDE), BF16),
            pltpu.VMEM((DEEP, L, WIDE), F32),
            pltpu.VMEM((DEEP, 2 * H, WIDE), BF16),
            pltpu.VMEM((DEEP, GROUP, CP), F32),
            pltpu.VMEM((DEEP + 1, L, CP), F32),
            pltpu.VMEM((DEEP, 2 * GROUP, CP), F32),
            pltpu.VMEM((n_row, CP, 2 * H), F32),
            pltpu.VMEM((n_col, H, CP), F32),
            pltpu.VMEM((H, H), F32),
            pltpu.VMEM((8, 2 * H), F32),
            pltpu.VMEM((n_row,) + rows[0].shape[1:], BF16),
            pltpu.VMEM((n_col,) + cols[0].shape[1:], BF16),
            pltpu.VMEM((PAR, H), F32),
        ],
        smem=2,
    )


def core_sum(chips, steps, recv, rows, cols, par, *outs):
    x_msgs, (y_msg, xy_msg, rows_out, cols_out, par_out) = outs[:chips - 1], outs[chips - 1:]
    n_row, n_col = rows.shape[0], cols.shape[0]
    total = par[...] + get_split(recv, n_row * 2 * L + n_col * L, HALF)
    par_out[...] = total
    put_split(xy_msg, 0, total)
    for c in range(n_row):
        value = rows[c] + recv[c * 2 * L:(c + 1) * 2 * L, :].astype(F32)
        step, inner = c // CELLS, c % CELLS
        if step == 0:
            rows_out[inner] = value
        else:
            x_msgs[step - 1][inner * 2 * L:(inner + 1) * 2 * L, :] = value.astype(BF16)
    for x_msg in x_msgs:
        put_split(x_msg, CELLS * 2 * L, total)
    for c in range(n_col):
        at = n_row * 2 * L + c * L
        value = cols[c] + recv[at:at + L, :].astype(F32)
        slot, inner = c // CELLS, c % CELLS
        to = (slot // 2) * CELLS + inner
        if slot % 2 == 0:
            cols_out[to] = value
        else:
            y_msg[to * L:(to + 1) * L, :] = value.astype(BF16)
    put_split(y_msg, steps * CELLS * L, total)


def near_sum(chips, steps, *refs):
    x_in, refs = refs[:chips - 1], refs[chips - 1:]
    xy_in, refs = refs[:chips - 1], refs[chips - 1:]
    (y_in, rows, cols, par), refs = refs[:4], refs[4:]
    rows_out, cols_out, par_out = refs[:3]
    z_msgs = refs[3:]
    total = par[...] + get_split(y_in, steps * CELLS * L, HALF)
    for ref in x_in:
        total = total + get_split(ref, CELLS * 2 * L, HALF)
    for ref in xy_in:
        total = total + get_split(ref, 0, HALF)
    par_out[...] = total
    for c in range(CELLS):
        value = rows[c]
        for ref in x_in:
            value = value + ref[c * 2 * L:(c + 1) * 2 * L, :].astype(F32)
        rows_out[c] = value
    for c in range(steps * CELLS):
        value = cols[c] + y_in[c * L:(c + 1) * L, :].astype(F32)
        step, inner = c // CELLS, c % CELLS
        if step == 0:
            cols_out[inner] = value
        else:
            z_msgs[step - 1][inner * L:(inner + 1) * L, :] = value.astype(BF16)
    for ref in z_msgs:
        put_split(ref, CELLS * L, total)


def far_sum(steps, *refs):
    z_in, refs = refs[:steps - 1], refs[steps - 1:]
    rows, cols, par, feats, cotangent, updated, grad_feats, par_out = refs
    total = par[...]
    for ref in z_in:
        total = total + get_split(ref, CELLS * L, HALF)
    par_out[...] = total
    for c in range(CELLS):
        value = cols[c]
        for ref in z_in:
            value = value + ref[c * L:(c + 1) * L, :].astype(F32)
        updated[c] = (feats[c].astype(F32) + rows[c, :L, :]).astype(BF16)
        grad_feats[c] = cotangent[c].astype(F32) + rows[c, L:, :] + value


def gather_halves(own, oth, first, bias1, dist, second, bias2, par):
    core = lax.rem(lax.axis_index("col"), 2)
    par[pl.ds(pl.multiple_of(core * HALF, HALF), HALF), :] = own[...]
    par[pl.ds(pl.multiple_of((1 - core) * HALF, HALF), HALF), :] = oth[...]
    first[...] = jnp.transpose(par[:2 * L, :])
    second[...] = par[2 * L:3 * L, :]
    bias1[...] = par[3 * L:3 * L + 1, :]
    dist[...] = par[3 * L + 1:3 * L + 2, :]
    bias2[...] = par[3 * L + 2:3 * L + 3, :]


def per_device(
    feats, coords, valid, pairs, pair_count, w_first, bias_first, dist_scale,
    w_second, bias_second, cotangent, rows_n, cols_n,
):
    steps, chips = rows_n // 2, cols_n // 2
    swap_y = [(i, i ^ 1) for i in range(rows_n)]
    swap_core = [(i, i ^ 1) for i in range(cols_n)]

    def along(n, d):
        return [(i, (i + 2 * d) % n) for i in range(n)]

    def diagonal(d):
        return [
            (r * cols_n + c, (r ^ 1) * cols_n + (c + 2 * d) % cols_n)
            for r in range(rows_n) for c in range(cols_n)
        ]

    extra = jnp.concatenate(
        [coords, valid.astype(BF16)[:, None], jnp.zeros((CELLS, 12, CP), BF16)], axis=1
    )
    col_own = jnp.concatenate([feats, extra], axis=1)
    row_own = jnp.concatenate([feats, cotangent, extra], axis=1)
    tiles = jnp.concatenate([pairs.reshape(-1), pair_count.reshape(-1)])
    col_pair = jnp.concatenate([col_own, lax.ppermute(col_own, "row", swap_y)], axis=0)
    row_parts = [row_own] + [
        lax.ppermute(row_own, "col", along(cols_n, -d)) for d in range(1, chips)
    ]
    col_parts = [col_pair] + [
        lax.ppermute(col_pair, "row", along(rows_n, -d)) for d in range(1, steps)
    ]
    other_tiles = lax.ppermute(tiles, "col", swap_core)
    row_parts += [lax.ppermute(p, "col", swap_core) for p in row_parts]
    col_parts += [lax.ppermute(p, "col", swap_core) for p in col_parts]
    send, rows, cols, par = pair_call(
        [tiles, other_tiles], row_parts, col_parts,
        [
            w_first, bias_first.reshape(1, H), dist_scale.reshape(1, H), w_second,
            jnp.pad(bias_second, (0, L)).reshape(1, 2 * L),
        ],
    )
    got = lax.ppermute(send, "col", swap_core)
    x_shape = ((CELLS * 2 * L + PAR, CP), BF16)
    keep = [((CELLS, 2 * L, CP), F32), ((steps * CELLS, L, CP), F32), ((HALF, H), F32)]
    outs = call(
        functools.partial(core_sum, chips, steps), "core_sum", [got, rows, cols, par],
        [x_shape] * (chips - 1)
        + [((steps * CELLS * L + PAR, CP), BF16), ((PAR, H), BF16)] + keep,
    )
    x_msgs, (y_msg, xy_msg, rows, cols, par) = outs[:chips - 1], outs[chips - 1:]
    y_in = lax.ppermute(y_msg, "row", swap_y)
    x_in = [lax.ppermute(m, "col", along(cols_n, d + 1)) for d, m in enumerate(x_msgs)]
    xy_in = [lax.ppermute(xy_msg, ("row", "col"), diagonal(d)) for d in range(1, chips)]
    keep[1] = ((CELLS, L, CP), F32)
    rows, cols, par, *z_msgs = call(
        functools.partial(near_sum, chips, steps), "near_sum",
        [*x_in, *xy_in, y_in, rows, cols, par],
        keep + [((CELLS * L + PAR, CP), BF16)] * (steps - 1),
    )
    z_in = [lax.ppermute(m, "row", along(rows_n, d + 1)) for d, m in enumerate(z_msgs)]
    updated, grad_feats, par = call(
        functools.partial(far_sum, steps), "far_sum",
        [*z_in, rows, cols, par, feats, cotangent],
        [((CELLS, L, CP), BF16), ((CELLS, L, CP), F32), ((HALF, H), F32)],
    )
    first, bias1, dist, second, bias2 = call(
        gather_halves, "gather_halves", [par, lax.ppermute(par, "col", swap_core)],
        [((H, 2 * L), F32), ((1, H), F32), ((1, H), F32), ((L, H), F32), ((1, H), F32)],
        [pltpu.VMEM((PAR, H), F32)],
    )
    return updated, grad_feats, first, bias1[0], dist[0], second, bias2[0, :L]


def solution(mesh):
    spread = P(("row", "col"))
    placed = (spread, spread, spread, P("row", "col"), P("row", "col"), P(), P(), P(), P(), P(), spread)
    return jax.shard_map(
        functools.partial(per_device, rows_n=mesh.shape["row"], cols_n=mesh.shape["col"]),
        mesh=mesh,
        in_specs=placed,
        out_specs=(spread, spread, P(), P(), P(), P(), P()),
        check_vma=False,
    )
```

```python
import functools
import jax
import jax.numpy as jnp
from jax import lax
from jax.experimental import pallas as pl
from jax.experimental.pallas import tpu as pltpu
from jax.sharding import PartitionSpec as P

L = 64
H = 128
CP = 128
GROUP = 16
WIDE = GROUP * CP
CELLS = 2
DEEP = 4
PAR = 224
HALF = PAR // 2
CHUNK = 8
QUAD = 4
NT = (((1,), (1,)), ((), ()))
NN = (((1,), (0,)), ((), ()))
F32 = jnp.float32
BF16 = jnp.bfloat16


def dot(a, b, dims=NN):
    return lax.dot_general(a, b, dims, preferred_element_type=F32)


def split(value):
    high = value.astype(BF16)
    return high, (value - high.astype(F32)).astype(BF16)


def put_split(ref, at, value):
    rows = value.shape[0]
    high, low = split(value)
    ref[at:at + rows, :] = high
    ref[at + rows:at + 2 * rows, :] = low


def get_split(ref, at, rows):
    return ref[at:at + rows, :].astype(F32) + ref[at + rows:at + 2 * rows, :].astype(F32)


def column(row, rows):
    return jnp.transpose(jnp.broadcast_to(row, (rows, row.shape[1])))


def pair_kernel(chips, steps, *refs):
    (own_ref, oth_ref), refs = refs[:2], refs[2:]
    row_refs, refs = refs[:2 * chips], refs[2 * chips:]
    col_refs, refs = refs[:2 * steps], refs[2 * steps:]
    (
        w1_ref, w2_ref, vec_ref,
        send_ref, keep_rows, keep_cols, keep_par,
        fixed, even, odd, pos, feat_b, rhs, y_s, slope_s, pm_s, x3_s, env_s, cot_s, split_s,
        racc, cacc, gw2, gds, r_ref, c_ref, par_ref,
    ) = refs
    me_row, me_col = lax.axis_index("row"), lax.axis_index("col")
    me_core = lax.rem(me_col, 2)
    half_rows = chips * CELLS
    half_cols = steps * 2 * CELLS
    for n, ref in enumerate(row_refs):
        r_ref[n * CELLS:(n + 1) * CELLS] = ref[...]
    for n, ref in enumerate(col_refs):
        c_ref[n * 2 * CELLS:(n + 1) * 2 * CELLS] = ref[...]
    slots = (own_ref.shape[0] - 1) // 2
    own_count, oth_count = own_ref[2 * slots], oth_ref[2 * slots]
    both_count = own_count + oth_count
    first_count = jnp.where(me_core == 0, own_count, oth_count)

    def place_row(cell):
        source, inner = cell // CELLS, lax.rem(cell, CELLS)
        step = lax.rem(source // 2 - me_col // 2 + chips, chips)
        return lax.rem(source + me_core, 2) * half_rows + step * CELLS + inner

    def place_col(cell):
        source, inner = cell // CELLS, lax.rem(cell, CELLS)
        step = lax.rem(source // 2 - me_row // 2 + steps, steps)
        return (step * 2 + lax.rem(source + me_row, 2)) * CELLS + inner

    def find(index):
        second = (index >= first_count).astype(jnp.int32)
        entry = index - second * first_count
        mine = second == me_core
        u = jnp.where(mine, own_ref[2 * entry], oth_ref[2 * entry])
        v = jnp.where(mine, own_ref[2 * entry + 1], oth_ref[2 * entry + 1])
        return place_row(u), place_col(v) + jnp.where(mine, 0, half_cols)

    lane = lax.broadcasted_iota(jnp.int32, (H, CP), 1)
    sub = lax.broadcasted_iota(jnp.int32, (8, CP), 0)
    lane2 = lax.broadcasted_iota(jnp.int32, (2 * H, CP), 1)
    zero8 = jnp.zeros((8, CP), F32)
    hot = (
        lax.broadcasted_iota(jnp.int32, (GROUP, WIDE), 1) // CP
        == lax.broadcasted_iota(jnp.int32, (GROUP, WIDE), 0)
    ).astype(F32).astype(BF16)
    for k in range(DEEP):
        rhs[k, 0:GROUP, :] = hot
        rhs[k, GROUP:2 * GROUP, :] = hot
        rhs[k, 2 * GROUP:3 * GROUP, :] = jnp.zeros((GROUP, WIDE), BF16)
    for k in range(DEEP):
        y_s[k, H:, :] = jnp.ones((GROUP, WIDE), BF16)
    for k in (DEEP - 2, DEEP - 1):
        y_s[k, 0:H, :] = jnp.zeros((H, WIDE), BF16)
    x3_s[DEEP - 2] = jnp.zeros((2 * H, WIDE), BF16)
    slope_s[DEEP - 1] = jnp.zeros((H, WIDE), BF16)
    pm_s[DEEP - 1] = jnp.zeros((L, WIDE), F32)
    env_s[DEEP - 1] = jnp.zeros((GROUP, CP), F32)
    cot_s[DEEP - 1] = jnp.zeros((L, CP), F32)
    racc[...] = jnp.zeros_like(racc)
    cacc[...] = jnp.zeros_like(cacc)
    gw2[...] = jnp.zeros_like(gw2)
    gds[...] = jnp.zeros_like(gds)
    b1_b = column(vec_ref[0:1, :], CP)
    ds_b = 0.5 * column(vec_ref[1:2, :], CP)
    b2_b = 0.5 * column(vec_ref[2:3, :], CP)[:L, :]
    ds_hi = ds_b.astype(BF16).astype(F32)
    ds_lo = ds_b - ds_hi
    w1 = w1_ref[...]
    w1r = w1[:, :L]
    w1f = 0.5 * w1.astype(F32)
    w1f = pltpu.roll(w1f, L, 1)
    ds_part = jnp.where(lane == 97, ds_lo, jnp.where((lane == 96) | (lane == 104), ds_hi, 0.0))
    fixed[...] = jnp.where(lane < L, w1f, ds_part)
    w2f = 0.5 * w2_ref[...].astype(F32)
    w2h = w2f.astype(BF16)
    b2_hi = b2_b.astype(BF16).astype(F32)
    b2_mid = (b2_b - b2_hi).astype(BF16).astype(F32)
    b2_part = jnp.where(lane[:L] == 0, b2_hi, jnp.where(lane[:L] == 1, b2_mid, jnp.where(lane[:L] == 2, b2_b - b2_hi - b2_mid, 0.0)))
    w2b = jnp.concatenate([w2h, b2_part[:, :GROUP].astype(BF16)], axis=1)
    w2t = jnp.transpose(w2f).astype(BF16)

    def forward_start(k, g):
        first = pl.multiple_of(g * GROUP, GROUP)
        rows = pl.ds(first, GROUP)
        sq = jnp.zeros((GROUP, CP), F32)
        for d in range(3):
            off = pos[d, rows, :] - pos[4, d:d + 1, :]
            sq = sq + off * off
        env_s[k] = pos[3, rows, :] * pos[4, 3:4, :] / ((1.0 + sq) * CP)
        sq_hi = sq.astype(BF16).astype(F32)
        split_s[k, 0:GROUP, :] = sq_hi
        split_s[k, GROUP:2 * GROUP, :] = sq - sq_hi
        for i in range(GROUP):
            at = slice(i * CP, (i + 1) * CP)
            hi_b = jnp.broadcast_to(split_s[k, i:i + 1, :], (8, CP))
            lo_b = jnp.broadcast_to(split_s[k, GROUP + i:GROUP + i + 1, :], (8, CP))
            rhs[k, 2 * GROUP:3 * GROUP, at] = jnp.concatenate([hi_b, lo_b], axis=0).astype(BF16)
        part = pltpu.roll((even if k % 2 == 0 else odd)[...], lax.rem(L - first + CP, CP), 1)
        mix = jnp.where((lane >= L) & (lane < 96), part, fixed[...]).astype(BF16)
        cot_s[k] = pltpu.roll(cot_s[DEEP], lax.rem(CP - first, CP), 1)
        return mix[:, :112]

    def lanes(c):
        return slice(c * CHUNK * CP, (c + 1) * CHUNK * CP)

    def first_layer(k, mix, c):
        return dot(mix, jnp.concatenate([feat_b[:, lanes(c)], rhs[k, :, lanes(c)]], axis=0))

    def forward_hidden(k, z, c):
        for i in range(CHUNK):
            at = slice((c * CHUNK + i) * CP, (c * CHUNK + i + 1) * CP)
            w = z[:, i * CP:(i + 1) * CP]
            p = 1.0 + jnp.tanh(w)
            y = (w * p).astype(BF16)
            y_s[k, 0:H, at] = y
            p = p.astype(BF16)
            slope_s[k, :, at] = p + y * (2.0 - p)
        pm_s[k, :, lanes(c)] = dot(w2b, y_s[k, :, lanes(c)])

    def back_message(k, c):
        for i in range(c * CHUNK, (c + 1) * CHUNK):
            at = slice(i * CP, (i + 1) * CP)
            w = pm_s[k, :, at]
            t = jnp.tanh(w)
            e = env_s[k, i:i + 1, :]
            p = (1.0 + t) * e
            y = w * p
            x3_s[k, L:2 * L, at] = y.astype(BF16)
            x3_s[k, 0:L, at] = ((p + y - y * t) * cot_s[k, :, i:i + 1]).astype(BF16)
        return dot(w2t, x3_s[k, 0:L, lanes(c)])

    def back_hidden(k, gh, total, c):
        for q in range(0, CHUNK, QUAD):
            some = None
            for i in range(q, q + QUAD):
                at = slice((c * CHUNK + i) * CP, (c * CHUNK + i + 1) * CP)
                inner = gh[:, i * CP:(i + 1) * CP].astype(BF16) * slope_s[k, :, at]
                x3_s[k, 2 * L:, at] = inner
                some = inner if some is None else some + inner
            total = total + some.astype(F32)
        return total

    def sums(k):
        both = jnp.concatenate([y_s[k, 0:H, :], rhs[k, GROUP:3 * GROUP, :]], axis=0)
        return dot(both, jnp.transpose(x3_s[k]))

    def put_sums(s, g, u):
        first = pl.multiple_of(g * GROUP, GROUP)
        gw2[...] += s[:H, :H]
        racc[u, pl.ds(first, GROUP), :] += s[H:H + GROUP]
        gds[...] += s[H + GROUP:H + 2 * GROUP]

    def half(k, g, v, g_sums, u_sums):
        back = (k - 1) % DEEP
        old = (k - 2) % DEEP
        chunks = GROUP // CHUNK
        mix = forward_start(k, g)
        total = cacc[v]
        s = None
        late = None
        s = sums(old)
        for c in range(chunks):
            z = first_layer(k, mix, c)
            gh = back_message(back, c)
            forward_hidden(k, z, c)
            total = back_hidden(back, gh, total, c)
        cacc[v] = total
        put_sums(s, g_sums, u_sums)

    def begin(u, v):
        a = 0.5 * (dot(w1r, r_ref[u, 0:L, :]) + b1_b)
        a_hi = a.astype(BF16).astype(F32)
        a_lo = pltpu.roll(a - a_hi, GROUP, 1)
        block = (lane // GROUP) % 2 == 0
        even[...] = jnp.where(block, a_hi, a_lo)
        odd[...] = jnp.where(block, a_lo, a_hi)
        cot_s[DEEP] = 0.5 * r_ref[u, L:2 * L, :].astype(F32)
        xu = r_ref[u, 2 * L:2 * L + 16, :].astype(F32)
        for d in range(4):
            pos[d] = column(xu[d:d + 1, :], CP)
        pos[4, 0:16, :] = c_ref[v, L:L + 16, :].astype(F32)
        fv = c_ref[v, 0:L, :]
        for i in range(GROUP):
            feat_b[:, i * CP:(i + 1) * CP] = fv

    parts = CP // GROUP // DEEP
    begins = jnp.where(me_core == 0, 0, both_count * parts // 2)
    ends = jnp.where(me_core == 0, both_count * parts // 2, both_count * parts)

    def unit(index, before):
        u_last, v_last, g_last = before
        u, v = find(index // parts)
        g = lax.rem(index, parts) * DEEP

        @pl.when((g == 0) | (index == begins))
        def _():
            begin(u, v)

        for k in range(DEEP):
            g_sums = g + k - 2 if k >= 2 else g_last + DEEP + k - 2
            half(k, g + k, v if k else v_last, g_sums, u if k >= 2 else u_last)
        return u, v, g

    zero = jnp.int32(0)
    u, v, g = lax.fori_loop(begins, ends, unit, (zero, zero, zero))
    total = cacc[v]
    for c in range(GROUP // CHUNK):
        total = back_hidden(DEEP - 1, back_message(DEEP - 1, c), total, c)
    cacc[v] = total
    put_sums(sums(DEEP - 2), g + DEEP - 2, u)
    put_sums(sums(DEEP - 1), g + DEEP - 1, u)

    w1t = 2.0 * jnp.transpose(w1f)
    ones = jnp.ones((GROUP, 8 * CP), BF16)
    par_ref[2 * L:3 * L, :] = jnp.transpose(gw2[...])[:L]
    par_ref[3 * L:, :] = jnp.zeros((PAR - 3 * L, H), F32)
    par_ref[3 * L + 1:3 * L + 2, :] = gds[0:1, H:] + gds[8:9, H:]

    def left_of(src, cells):
        feats = jnp.concatenate([src[c, 0:L, :] for c in cells], axis=1)
        return jnp.concatenate([feats, ones[:, :len(cells) * CP]], axis=0)

    def row_block(start, count, put):
        cells = [start + n for n in range(count)]
        high, low = split(jnp.concatenate([racc[c, :, H:] for c in cells], axis=0))
        values = dot(w_row, high, NT) + dot(w_row, low, NT)
        for n, c in enumerate(cells):
            put(c, values[:, n * CP:(n + 1) * CP], jnp.transpose(racc[c, :, :H])[L:])
        left = left_of(r_ref, cells)
        return dot(left, high) + dot(left, low)

    def col_block(start, count, put):
        cells = [start + n for n in range(count)]
        high, low = split(jnp.concatenate([cacc[c] for c in cells], axis=1))
        values = dot(w_col, high) + dot(w_col, low)
        for n, c in enumerate(cells):
            put(c, values[:, n * CP:(n + 1) * CP])
        left = left_of(c_ref, cells)
        return dot(left, high, NT) + dot(left, low, NT)

    def keep_row(c, value, message):
        keep_rows[c, 0:L, :] = message
        keep_rows[c, L:2 * L, :] = value

    def send_row(c, value, message):
        at = pl.multiple_of((c - half_rows) * 2 * L, 2 * L)
        send_ref[pl.ds(at, L), :] = message.astype(BF16)
        send_ref[pl.ds(at + L, L), :] = value.astype(BF16)

    def keep_col(c, value):
        keep_cols[c] = value

    def send_col(c, value):
        at = pl.multiple_of(half_rows * 2 * L + (c - half_cols) * L, L)
        send_ref[pl.ds(at, L), :] = value.astype(BF16)

    def sweep(block, start, total, count, put):
        return lax.fori_loop(
            0, total // count,
            lambda n, part: part + block(start + n * count, count, put),
            jnp.zeros((L + GROUP, H), F32),
        )

    w_row, w_col = w1t[L:].astype(BF16), w1t[:L].astype(BF16)
    first = sweep(row_block, 0, half_rows, 4, keep_row)
    first = first + sweep(row_block, half_rows, half_rows, 4, send_row)
    par_ref[0:L, :] = first[:L]
    par_ref[3 * L:3 * L + 1, :] = first[L:L + 1]
    bias2 = jnp.zeros((1, H), F32)
    for c in range(2 * half_rows):
        bias2 = bias2 + jnp.sum(racc[c, :, :H], axis=0, keepdims=True)
    par_ref[3 * L + 2:3 * L + 3, :] = bias2
    first = sweep(col_block, 0, half_cols, 8, keep_col)
    first = first + sweep(col_block, half_cols, half_cols, 8, send_col)
    par_ref[L:2 * L, :] = first[:L]
    keep_par[...] = par_ref[pl.ds(pl.multiple_of(me_core * HALF, HALF), HALF), :]
    put_split(send_ref, half_rows * 2 * L + half_cols * L,
              par_ref[pl.ds(pl.multiple_of((1 - me_core) * HALF, HALF), HALF), :])


VM = pl.BlockSpec(memory_space=pltpu.VMEM)
SM = pl.BlockSpec(memory_space=pltpu.SMEM)


def call(kernel, name, ins, outs, scratch=(), smem=0, limit=48):
    return pl.pallas_call(
        kernel,
        out_shape=tuple(jax.ShapeDtypeStruct(s, d) for s, d in outs),
        in_specs=[SM] * smem + [VM] * (len(ins) - smem),
        out_specs=(VM,) * len(outs),
        scratch_shapes=list(scratch),
        compiler_params=pltpu.CompilerParams(vmem_limit_bytes=limit * 1024 * 1024),
        name=name,
    )(*ins)


def pair_call(lists, rows, cols, weights):
    chips, steps = len(rows) // 2, len(cols) // 2
    n_row, n_col = 2 * chips * CELLS, 4 * steps * CELLS
    sent = n_row // 2 * 2 * L + n_col // 2 * L + PAR
    return call(
        functools.partial(pair_kernel, chips, steps),
        "pair_tiles",
        [*lists, *rows, *cols, *weights],
        [
            ((sent, CP), BF16),
            ((n_row // 2, 2 * L, CP), F32),
            ((n_col // 2, L, CP), F32),
            ((HALF, H), F32),
        ],
        [
            pltpu.VMEM((H, CP), F32),
            pltpu.VMEM((H, CP), F32),
            pltpu.VMEM((H, CP), F32),
            pltpu.VMEM((5, CP, CP), F32),
            pltpu.VMEM((L, WIDE), BF16),
            pltpu.VMEM((DEEP, 3 * GROUP, WIDE), BF16),
            pltpu.VMEM((DEEP, H + GROUP, WIDE), BF16),
            pltpu.VMEM((DEEP, H, WIDE), BF16),
            pltpu.VMEM((DEEP, L, WIDE), F32),
            pltpu.VMEM((DEEP, 2 * H, WIDE), BF16),
            pltpu.VMEM((DEEP, GROUP, CP), F32),
            pltpu.VMEM((DEEP + 1, L, CP), F32),
            pltpu.VMEM((DEEP, 2 * GROUP, CP), F32),
            pltpu.VMEM((n_row, CP, 2 * H), F32),
            pltpu.VMEM((n_col, H, CP), F32),
            pltpu.VMEM((H, H), F32),
            pltpu.VMEM((GROUP, 2 * H), F32),
            pltpu.VMEM((n_row,) + rows[0].shape[1:], BF16),
            pltpu.VMEM((n_col,) + cols[0].shape[1:], BF16),
            pltpu.VMEM((PAR, H), F32),
        ],
        smem=2,
    )


def core_sum(chips, steps, recv, rows, cols, par, *outs):
    x_msgs, (y_msg, xy_msg, rows_out, cols_out, par_out) = outs[:chips - 1], outs[chips - 1:]
    n_row, n_col = rows.shape[0], cols.shape[0]
    total = par[...] + get_split(recv, n_row * 2 * L + n_col * L, HALF)
    par_out[...] = total
    put_split(xy_msg, 0, total)
    for c in range(n_row):
        value = rows[c] + recv[c * 2 * L:(c + 1) * 2 * L, :].astype(F32)
        step, inner = c // CELLS, c % CELLS
        if step == 0:
            rows_out[inner] = value
        else:
            x_msgs[step - 1][inner * 2 * L:(inner + 1) * 2 * L, :] = value.astype(BF16)
    for x_msg in x_msgs:
        put_split(x_msg, CELLS * 2 * L, total)
    for c in range(n_col):
        at = n_row * 2 * L + c * L
        value = cols[c] + recv[at:at + L, :].astype(F32)
        slot, inner = c // CELLS, c % CELLS
        to = (slot // 2) * CELLS + inner
        if slot % 2 == 0:
            cols_out[to] = value
        else:
            y_msg[to * L:(to + 1) * L, :] = value.astype(BF16)
    put_split(y_msg, steps * CELLS * L, total)


def near_sum(chips, steps, *refs):
    x_in, refs = refs[:chips - 1], refs[chips - 1:]
    xy_in, refs = refs[:chips - 1], refs[chips - 1:]
    (y_in, rows, cols, par), refs = refs[:4], refs[4:]
    rows_out, cols_out, par_out = refs[:3]
    z_msgs = refs[3:]
    total = par[...] + get_split(y_in, steps * CELLS * L, HALF)
    for ref in x_in:
        total = total + get_split(ref, CELLS * 2 * L, HALF)
    for ref in xy_in:
        total = total + get_split(ref, 0, HALF)
    par_out[...] = total
    for c in range(CELLS):
        value = rows[c]
        for ref in x_in:
            value = value + ref[c * 2 * L:(c + 1) * 2 * L, :].astype(F32)
        rows_out[c] = value
    for c in range(steps * CELLS):
        value = cols[c] + y_in[c * L:(c + 1) * L, :].astype(F32)
        step, inner = c // CELLS, c % CELLS
        if step == 0:
            cols_out[inner] = value
        else:
            z_msgs[step - 1][inner * L:(inner + 1) * L, :] = value.astype(BF16)
    for ref in z_msgs:
        ref[CELLS * L:, :] = total.astype(BF16)


def far_par(steps, *refs):
    z_in, (par, par_out) = refs[:steps - 1], refs[steps - 1:]
    total = par[...]
    for ref in z_in:
        total = total + ref[CELLS * L:, :].astype(F32)
    par_out[...] = total


def far_cells(steps, *refs):
    z_in, refs = refs[:steps - 1], refs[steps - 1:]
    rows, cols, own, updated, grad_feats = refs
    for c in range(CELLS):
        value = cols[c]
        for ref in z_in:
            value = value + ref[c * L:(c + 1) * L, :].astype(F32)
        updated[c] = (own[c, 0:L, :].astype(F32) + rows[c, :L, :]).astype(BF16)
        grad_feats[c] = own[c, L:2 * L, :].astype(F32) + rows[c, L:, :] + value


def gather_halves(own, oth, first, bias1, dist, second, bias2, par):
    core = lax.rem(lax.axis_index("col"), 2)
    par[pl.ds(pl.multiple_of(core * HALF, HALF), HALF), :] = own[...]
    par[pl.ds(pl.multiple_of((1 - core) * HALF, HALF), HALF), :] = oth[...]
    first[...] = jnp.transpose(par[:2 * L, :])
    second[...] = par[2 * L:3 * L, :]
    bias1[...] = par[3 * L:3 * L + 1, :]
    dist[...] = par[3 * L + 1:3 * L + 2, :]
    bias2[...] = par[3 * L + 2:3 * L + 3, :L]


def per_device(
    feats, coords, valid, pairs, pair_count, w_first, bias_first, dist_scale,
    w_second, bias_second, cotangent, rows_n, cols_n,
):
    steps, chips = rows_n // 2, cols_n // 2
    swap_y = [(i, i ^ 1) for i in range(rows_n)]
    swap_core = [(i, i ^ 1) for i in range(cols_n)]

    def along(n, d):
        return [(i, (i + 2 * d) % n) for i in range(n)]

    def diagonal(d):
        return [
            (r * cols_n + c, (r ^ 1) * cols_n + (c + 2 * d) % cols_n)
            for r in range(rows_n) for c in range(cols_n)
        ]

    extra = jnp.concatenate(
        [coords, valid.astype(BF16)[:, None], jnp.zeros((CELLS, 12, CP), BF16)], axis=1
    )
    col_own = jnp.concatenate([feats, extra], axis=1)
    col_own, late = lax.optimization_barrier((col_own, cotangent))
    row_own = jnp.concatenate([col_own[:, :L], late, col_own[:, L:]], axis=1)
    tiles = jnp.concatenate([pairs.reshape(-1), pair_count.reshape(-1)])
    vectors = jnp.stack([bias_first, dist_scale, jnp.pad(bias_second, (0, L)), bias_first])
    col_y = lax.ppermute(col_own, "row", swap_y)
    col_y, vectors = lax.optimization_barrier((col_y, vectors))
    col_pair = jnp.concatenate([col_own, col_y], axis=0)
    row_parts = [row_own] + [
        lax.ppermute(row_own, "col", along(cols_n, -d)) for d in range(1, chips)
    ]
    col_parts = [col_pair] + [
        lax.ppermute(col_pair, "row", along(rows_n, -d)) for d in range(1, steps)
    ]
    other_tiles = lax.ppermute(tiles, "col", swap_core)
    row_swapped = [lax.ppermute(p, "col", swap_core) for p in row_parts]
    col_parts[-1], other_tiles, *row_swapped = lax.optimization_barrier(
        (col_parts[-1], other_tiles, *row_swapped)
    )
    row_parts += row_swapped
    col_parts += [lax.ppermute(p, "col", swap_core) for p in col_parts]
    send, rows, cols, par = pair_call(
        [tiles, other_tiles], row_parts, col_parts,
        [w_first, w_second, vectors],
    )
    got = lax.ppermute(send, "col", swap_core)
    x_shape = ((CELLS * 2 * L + PAR, CP), BF16)
    keep = [((CELLS, 2 * L, CP), F32), ((steps * CELLS, L, CP), F32), ((HALF, H), F32)]
    outs = call(
        functools.partial(core_sum, chips, steps), "core_sum", [got, rows, cols, par],
        [x_shape] * (chips - 1)
        + [((steps * CELLS * L + PAR, CP), BF16), ((PAR, H), BF16)] + keep,
    )
    x_msgs, (y_msg, xy_msg, rows, cols, par) = outs[:chips - 1], outs[chips - 1:]
    y_in = lax.ppermute(y_msg, "row", swap_y)
    x_in = [lax.ppermute(m, "col", along(cols_n, d + 1)) for d, m in enumerate(x_msgs)]
    xy_in = [lax.ppermute(xy_msg, ("row", "col"), diagonal(d)) for d in range(1, chips)]
    keep[1] = ((CELLS, L, CP), F32)
    rows, cols, par, *z_msgs = call(
        functools.partial(near_sum, chips, steps), "near_sum",
        [*x_in, *xy_in, y_in, rows, cols, par],
        keep + [((CELLS * L + HALF, CP), BF16)] * (steps - 1),
    )
    z_in = [lax.ppermute(m, "row", along(rows_n, d + 1)) for d, m in enumerate(z_msgs)]
    par, = call(
        functools.partial(far_par, steps), "far_par", [*z_in, par], [((HALF, H), F32)], limit=16
    )
    par_in = lax.ppermute(par, "col", swap_core)
    updated, grad_feats = call(
        functools.partial(far_cells, steps), "far_cells",
        [*z_in, rows, cols, row_own],
        [((CELLS, L, CP), BF16), ((CELLS, L, CP), F32)], limit=16,
    )
    first, bias1, dist, second, bias2 = call(
        gather_halves, "gather_halves", [par, par_in],
        [((H, 2 * L), F32), ((1, H), F32), ((1, H), F32), ((L, H), F32), ((1, L), F32)],
        [pltpu.VMEM((PAR, H), F32)],
    )
    return updated, grad_feats, first, bias1[0], dist[0], second, bias2[0]


def solution(mesh):
    spread = P(("row", "col"))
    placed = (spread, spread, spread, P("row", "col"), P("row", "col"), P(), P(), P(), P(), P(), spread)
    return jax.shard_map(
        functools.partial(per_device, rows_n=mesh.shape["row"], cols_n=mesh.shape["col"]),
        mesh=mesh,
        in_specs=placed,
        out_specs=(spread, spread, P(), P(), P(), P(), P()),
        check_vma=False,
    )
```

```python
import functools
import jax
import jax.numpy as jnp
from jax import lax
from jax.experimental import pallas as pl
from jax.experimental.pallas import tpu as pltpu
from jax.sharding import PartitionSpec as P

L = 64
H = 128
CP = 128
GROUP = 16
WIDE = GROUP * CP
CELLS = 2
DEEP = 4
PAR = 224
HALF = PAR // 2
CHUNK = 8
QUAD = 8
NT = (((1,), (1,)), ((), ()))
NN = (((1,), (0,)), ((), ()))
F32 = jnp.float32
BF16 = jnp.bfloat16


def dot(a, b, dims=NN):
    return lax.dot_general(a, b, dims, preferred_element_type=F32)


def split(value):
    high = value.astype(BF16)
    return high, (value - high.astype(F32)).astype(BF16)


def put_split(ref, at, value):
    rows = value.shape[0]
    high, low = split(value)
    ref[at:at + rows, :] = high
    ref[at + rows:at + 2 * rows, :] = low


def get_split(ref, at, rows):
    return ref[at:at + rows, :].astype(F32) + ref[at + rows:at + 2 * rows, :].astype(F32)


def column(row, rows):
    return jnp.transpose(jnp.broadcast_to(row, (rows, row.shape[1])))


def pair_kernel(chips, steps, *refs):
    (own_ref, oth_ref), refs = refs[:2], refs[2:]
    row_refs, refs = refs[:2 * chips], refs[2 * chips:]
    col_refs, refs = refs[:2 * steps], refs[2 * steps:]
    (
        w1_ref, w2_ref, vec_ref,
        send_ref, keep_rows, keep_cols, keep_par,
        fixed, even, odd, pos, feat_b, rhs, y_s, slope_s, pm_s, x3_s, env_s, cot_s, split_s,
        racc, cacc, gw2, gds, r_ref, c_ref, par_ref,
    ) = refs
    me_row, me_col = lax.axis_index("row"), lax.axis_index("col")
    me_core = lax.rem(me_col, 2)
    half_rows = chips * CELLS
    half_cols = steps * 2 * CELLS
    for n, ref in enumerate(row_refs):
        r_ref[n * CELLS:(n + 1) * CELLS] = ref[...]
    for n, ref in enumerate(col_refs):
        c_ref[n * 2 * CELLS:(n + 1) * 2 * CELLS] = ref[...]
    slots = (own_ref.shape[0] - 1) // 2
    own_count, oth_count = own_ref[2 * slots], oth_ref[2 * slots]
    both_count = own_count + oth_count
    first_count = jnp.where(me_core == 0, own_count, oth_count)

    def place_row(cell):
        source, inner = cell // CELLS, lax.rem(cell, CELLS)
        step = lax.rem(source // 2 - me_col // 2 + chips, chips)
        return lax.rem(source + me_core, 2) * half_rows + step * CELLS + inner

    def place_col(cell):
        source, inner = cell // CELLS, lax.rem(cell, CELLS)
        step = lax.rem(source // 2 - me_row // 2 + steps, steps)
        return (step * 2 + lax.rem(source + me_row, 2)) * CELLS + inner

    def find(index):
        second = (index >= first_count).astype(jnp.int32)
        entry = index - second * first_count
        mine = second == me_core
        u = jnp.where(mine, own_ref[2 * entry], oth_ref[2 * entry])
        v = jnp.where(mine, own_ref[2 * entry + 1], oth_ref[2 * entry + 1])
        return place_row(u), place_col(v) + jnp.where(mine, 0, half_cols)

    lane = lax.broadcasted_iota(jnp.int32, (H, CP), 1)
    sub = lax.broadcasted_iota(jnp.int32, (8, CP), 0)
    lane2 = lax.broadcasted_iota(jnp.int32, (2 * H, CP), 1)
    zero8 = jnp.zeros((8, CP), F32)
    hot = (
        lax.broadcasted_iota(jnp.int32, (GROUP, WIDE), 1) // CP
        == lax.broadcasted_iota(jnp.int32, (GROUP, WIDE), 0)
    ).astype(F32).astype(BF16)
    for k in range(DEEP):
        rhs[k, 0:GROUP, :] = hot
        rhs[k, GROUP:2 * GROUP, :] = hot
        rhs[k, 2 * GROUP:3 * GROUP, :] = jnp.zeros((GROUP, WIDE), BF16)
    for k in range(DEEP):
        y_s[k, H:, :] = jnp.ones((GROUP, WIDE), BF16)
    for k in (DEEP - 2, DEEP - 1):
        y_s[k, 0:H, :] = jnp.zeros((H, WIDE), BF16)
    x3_s[DEEP - 2] = jnp.zeros((2 * H, WIDE), BF16)
    slope_s[DEEP - 1] = jnp.zeros((H, WIDE), BF16)
    pm_s[DEEP - 1] = jnp.zeros((L, WIDE), F32)
    env_s[DEEP - 1] = jnp.zeros((GROUP, CP), F32)
    cot_s[DEEP - 1] = jnp.zeros((L, CP), F32)
    racc[...] = jnp.zeros_like(racc)
    cacc[...] = jnp.zeros_like(cacc)
    gw2[...] = jnp.zeros_like(gw2)
    gds[...] = jnp.zeros_like(gds)
    b1_b = column(vec_ref[0:1, :], CP)
    ds_b = 0.5 * column(vec_ref[1:2, :], CP)
    b2_b = 0.5 * column(vec_ref[2:3, :], CP)[:L, :]
    ds_hi = ds_b.astype(BF16).astype(F32)
    ds_lo = ds_b - ds_hi
    w1 = w1_ref[...]
    w1r = w1[:, :L]
    w1f = 0.5 * w1.astype(F32)
    w1f = pltpu.roll(w1f, L, 1)
    ds_part = jnp.where(lane == 97, ds_lo, jnp.where((lane == 96) | (lane == 104), ds_hi, 0.0))
    fixed[...] = jnp.where(lane < L, w1f, ds_part)
    w2f = 0.5 * w2_ref[...].astype(F32)
    w2h = w2f.astype(BF16)
    b2_hi = b2_b.astype(BF16).astype(F32)
    b2_mid = (b2_b - b2_hi).astype(BF16).astype(F32)
    b2_part = jnp.where(lane[:L] == 0, b2_hi, jnp.where(lane[:L] == 1, b2_mid, jnp.where(lane[:L] == 2, b2_b - b2_hi - b2_mid, 0.0)))
    w2b = jnp.concatenate([w2h, b2_part[:, :GROUP].astype(BF16)], axis=1)
    w2t = jnp.transpose(w2f).astype(BF16)

    def forward_start(k, g):
        first = pl.multiple_of(g * GROUP, GROUP)
        rows = pl.ds(first, GROUP)
        sq = jnp.zeros((GROUP, CP), F32)
        for d in range(3):
            off = pos[d, rows, :] - pos[4, d:d + 1, :]
            sq = sq + off * off
        env_s[k] = pos[3, rows, :] * pos[4, 3:4, :] / ((1.0 + sq) * CP)
        sq_hi = sq.astype(BF16).astype(F32)
        split_s[k, 0:GROUP, :] = sq_hi
        split_s[k, GROUP:2 * GROUP, :] = sq - sq_hi
        for i in range(GROUP):
            at = slice(i * CP, (i + 1) * CP)
            hi_b = jnp.broadcast_to(split_s[k, i:i + 1, :], (8, CP))
            lo_b = jnp.broadcast_to(split_s[k, GROUP + i:GROUP + i + 1, :], (8, CP))
            rhs[k, 2 * GROUP:3 * GROUP, at] = jnp.concatenate([hi_b, lo_b], axis=0).astype(BF16)
        part = pltpu.roll((even if k % 2 == 0 else odd)[...], lax.rem(L - first + CP, CP), 1)
        mix = jnp.where((lane >= L) & (lane < 96), part, fixed[...]).astype(BF16)
        cot_s[k] = pltpu.roll(cot_s[DEEP], lax.rem(CP - first, CP), 1)
        return mix[:, :112]

    def lanes(c):
        return slice(c * CHUNK * CP, (c + 1) * CHUNK * CP)

    def first_layer(k, mix, c):
        return dot(mix, jnp.concatenate([feat_b[:, lanes(c)], rhs[k, :, lanes(c)]], axis=0))

    def forward_hidden(k, z, c):
        for i in range(CHUNK):
            at = slice((c * CHUNK + i) * CP, (c * CHUNK + i + 1) * CP)
            w = z[:, i * CP:(i + 1) * CP]
            p = 1.0 + jnp.tanh(w)
            y = (w * p).astype(BF16)
            y_s[k, 0:H, at] = y
            p = p.astype(BF16)
            slope_s[k, :, at] = p + y * (2.0 - p)
        pm_s[k, :, lanes(c)] = dot(w2b, y_s[k, :, lanes(c)])

    def back_message(k, c):
        for i in range(c * CHUNK, (c + 1) * CHUNK):
            at = slice(i * CP, (i + 1) * CP)
            w = pm_s[k, :, at]
            t = jnp.tanh(w)
            e = env_s[k, i:i + 1, :]
            p = (1.0 + t) * e
            y = w * p
            x3_s[k, L:2 * L, at] = y.astype(BF16)
            x3_s[k, 0:L, at] = ((p + y - y * t) * cot_s[k, :, i:i + 1]).astype(BF16)
        return dot(w2t, x3_s[k, 0:L, lanes(c)])

    def back_hidden(k, gh, total, c):
        for q in range(0, CHUNK, QUAD):
            some = None
            for i in range(q, q + QUAD):
                at = slice((c * CHUNK + i) * CP, (c * CHUNK + i + 1) * CP)
                inner = gh[:, i * CP:(i + 1) * CP].astype(BF16) * slope_s[k, :, at]
                x3_s[k, 2 * L:, at] = inner
                some = inner if some is None else some + inner
            total = total + some.astype(F32)
        return total

    def sums(k):
        both = jnp.concatenate([y_s[k, 0:H, :], rhs[k, GROUP:3 * GROUP, :]], axis=0)
        return dot(both, jnp.transpose(x3_s[k]))

    def put_sums(s, g, u):
        first = pl.multiple_of(g * GROUP, GROUP)
        gw2[...] += s[:H, :H]
        racc[u, pl.ds(first, GROUP), :] += s[H:H + GROUP]
        gds[...] += s[H + GROUP:H + 2 * GROUP]

    def half(k, g, v, g_sums, u_sums):
        back = (k - 1) % DEEP
        old = (k - 2) % DEEP
        chunks = GROUP // CHUNK
        mix = forward_start(k, g)
        total = cacc[v]
        s = None
        late = None
        s = sums(old)
        z = first_layer(k, mix, 0)
        gh = back_message(back, 0)
        for c in range(chunks):
            z_next = first_layer(k, mix, c + 1) if c + 1 < chunks else None
            forward_hidden(k, z, c)
            gh_next = back_message(back, c + 1) if c + 1 < chunks else None
            total = back_hidden(back, gh, total, c)
            z, gh = z_next, gh_next
        cacc[v] = total
        put_sums(s, g_sums, u_sums)

    def begin(u, v):
        a = 0.5 * (dot(w1r, r_ref[u, 0:L, :]) + b1_b)
        a_hi = a.astype(BF16).astype(F32)
        a_lo = pltpu.roll(a - a_hi, GROUP, 1)
        block = (lane // GROUP) % 2 == 0
        even[...] = jnp.where(block, a_hi, a_lo)
        odd[...] = jnp.where(block, a_lo, a_hi)
        cot_s[DEEP] = 0.5 * r_ref[u, L:2 * L, :].astype(F32)
        xu = r_ref[u, 2 * L:2 * L + 16, :].astype(F32)
        for d in range(4):
            pos[d] = column(xu[d:d + 1, :], CP)
        pos[4, 0:16, :] = c_ref[v, L:L + 16, :].astype(F32)
        fv = c_ref[v, 0:L, :]
        for i in range(GROUP):
            feat_b[:, i * CP:(i + 1) * CP] = fv

    parts = CP // GROUP // DEEP
    begins = jnp.where(me_core == 0, 0, both_count * parts // 2)
    ends = jnp.where(me_core == 0, both_count * parts // 2, both_count * parts)

    def unit(index, before):
        u_last, v_last, g_last = before
        u, v = find(index // parts)
        g = lax.rem(index, parts) * DEEP

        @pl.when((g == 0) | (index == begins))
        def _():
            begin(u, v)

        for k in range(DEEP):
            g_sums = g + k - 2 if k >= 2 else g_last + DEEP + k - 2
            half(k, g + k, v if k else v_last, g_sums, u if k >= 2 else u_last)
        return u, v, g

    zero = jnp.int32(0)
    u, v, g = lax.fori_loop(begins, ends, unit, (zero, zero, zero))
    total = cacc[v]
    for c in range(GROUP // CHUNK):
        total = back_hidden(DEEP - 1, back_message(DEEP - 1, c), total, c)
    cacc[v] = total
    put_sums(sums(DEEP - 2), g + DEEP - 2, u)
    put_sums(sums(DEEP - 1), g + DEEP - 1, u)

    w1t = 2.0 * jnp.transpose(w1f)
    ones = jnp.ones((GROUP, 8 * CP), BF16)
    par_ref[2 * L:3 * L, :] = jnp.transpose(gw2[...])[:L]
    par_ref[3 * L:, :] = jnp.zeros((PAR - 3 * L, H), F32)
    par_ref[3 * L + 1:3 * L + 2, :] = gds[0:1, H:] + gds[8:9, H:]

    def left_of(src, cells):
        feats = jnp.concatenate([src[c, 0:L, :] for c in cells], axis=1)
        return jnp.concatenate([feats, ones[:, :len(cells) * CP]], axis=0)

    def row_block(start, count, put):
        cells = [start + n for n in range(count)]
        high, low = split(jnp.concatenate([racc[c, :, H:] for c in cells], axis=0))
        values = dot(w_row, high, NT) + dot(w_row, low, NT)
        for n, c in enumerate(cells):
            put(c, values[:, n * CP:(n + 1) * CP], jnp.transpose(racc[c, :, :H])[L:])
        left = left_of(r_ref, cells)
        return dot(left, high) + dot(left, low)

    def col_block(start, count, put):
        cells = [start + n for n in range(count)]
        high, low = split(jnp.concatenate([cacc[c] for c in cells], axis=1))
        values = dot(w_col, high) + dot(w_col, low)
        for n, c in enumerate(cells):
            put(c, values[:, n * CP:(n + 1) * CP])
        left = left_of(c_ref, cells)
        return dot(left, high, NT) + dot(left, low, NT)

    def keep_row(c, value, message):
        keep_rows[c, 0:L, :] = message
        keep_rows[c, L:2 * L, :] = value

    def send_row(c, value, message):
        at = pl.multiple_of((c - half_rows) * 2 * L, 2 * L)
        send_ref[pl.ds(at, L), :] = message.astype(BF16)
        send_ref[pl.ds(at + L, L), :] = value.astype(BF16)

    def keep_col(c, value):
        keep_cols[c] = value

    def send_col(c, value):
        at = pl.multiple_of(half_rows * 2 * L + (c - half_cols) * L, L)
        send_ref[pl.ds(at, L), :] = value.astype(BF16)

    def sweep(block, start, total, count, put):
        return lax.fori_loop(
            0, total // count,
            lambda n, part: part + block(start + n * count, count, put),
            jnp.zeros((L + GROUP, H), F32),
        )

    w_row, w_col = w1t[L:].astype(BF16), w1t[:L].astype(BF16)
    first = sweep(row_block, 0, half_rows, 4, keep_row)
    first = first + sweep(row_block, half_rows, half_rows, 4, send_row)
    par_ref[0:L, :] = first[:L]
    par_ref[3 * L:3 * L + 1, :] = first[L:L + 1]
    bias2 = jnp.zeros((1, H), F32)
    for c in range(2 * half_rows):
        bias2 = bias2 + jnp.sum(racc[c, :, :H], axis=0, keepdims=True)
    par_ref[3 * L + 2:3 * L + 3, :] = bias2
    first = sweep(col_block, 0, half_cols, 8, keep_col)
    first = first + sweep(col_block, half_cols, half_cols, 8, send_col)
    par_ref[L:2 * L, :] = first[:L]
    keep_par[...] = par_ref[pl.ds(pl.multiple_of(me_core * HALF, HALF), HALF), :]
    put_split(send_ref, half_rows * 2 * L + half_cols * L,
              par_ref[pl.ds(pl.multiple_of((1 - me_core) * HALF, HALF), HALF), :])


VM = pl.BlockSpec(memory_space=pltpu.VMEM)
SM = pl.BlockSpec(memory_space=pltpu.SMEM)


def call(kernel, name, ins, outs, scratch=(), smem=0, limit=48):
    return pl.pallas_call(
        kernel,
        out_shape=tuple(jax.ShapeDtypeStruct(s, d) for s, d in outs),
        in_specs=[SM] * smem + [VM] * (len(ins) - smem),
        out_specs=(VM,) * len(outs),
        scratch_shapes=list(scratch),
        compiler_params=pltpu.CompilerParams(vmem_limit_bytes=limit * 1024 * 1024),
        name=name,
    )(*ins)


def pair_call(lists, rows, cols, weights):
    chips, steps = len(rows) // 2, len(cols) // 2
    n_row, n_col = 2 * chips * CELLS, 4 * steps * CELLS
    sent = n_row // 2 * 2 * L + n_col // 2 * L + PAR
    return call(
        functools.partial(pair_kernel, chips, steps),
        "pair_tiles",
        [*lists, *rows, *cols, *weights],
        [
            ((sent, CP), BF16),
            ((n_row // 2, 2 * L, CP), F32),
            ((n_col // 2, L, CP), F32),
            ((HALF, H), F32),
        ],
        [
            pltpu.VMEM((H, CP), F32),
            pltpu.VMEM((H, CP), F32),
            pltpu.VMEM((H, CP), F32),
            pltpu.VMEM((5, CP, CP), F32),
            pltpu.VMEM((L, WIDE), BF16),
            pltpu.VMEM((DEEP, 3 * GROUP, WIDE), BF16),
            pltpu.VMEM((DEEP, H + GROUP, WIDE), BF16),
            pltpu.VMEM((DEEP, H, WIDE), BF16),
            pltpu.VMEM((DEEP, L, WIDE), F32),
            pltpu.VMEM((DEEP, 2 * H, WIDE), BF16),
            pltpu.VMEM((DEEP, GROUP, CP), F32),
            pltpu.VMEM((DEEP + 1, L, CP), F32),
            pltpu.VMEM((DEEP, 2 * GROUP, CP), F32),
            pltpu.VMEM((n_row, CP, 2 * H), F32),
            pltpu.VMEM((n_col, H, CP), F32),
            pltpu.VMEM((H, H), F32),
            pltpu.VMEM((GROUP, 2 * H), F32),
            pltpu.VMEM((n_row,) + rows[0].shape[1:], BF16),
            pltpu.VMEM((n_col,) + cols[0].shape[1:], BF16),
            pltpu.VMEM((PAR, H), F32),
        ],
        smem=2,
    )


def core_sum(chips, steps, recv, rows, cols, par, *outs):
    x_msgs, (y_msg, xy_msg, rows_out, cols_out, par_out) = outs[:chips - 1], outs[chips - 1:]
    n_row, n_col = rows.shape[0], cols.shape[0]
    total = par[...] + get_split(recv, n_row * 2 * L + n_col * L, HALF)
    par_out[...] = total
    put_split(xy_msg, 0, total)
    for c in range(n_row):
        value = rows[c] + recv[c * 2 * L:(c + 1) * 2 * L, :].astype(F32)
        step, inner = c // CELLS, c % CELLS
        if step == 0:
            rows_out[inner] = value
        else:
            x_msgs[step - 1][inner * 2 * L:(inner + 1) * 2 * L, :] = value.astype(BF16)
    for x_msg in x_msgs:
        put_split(x_msg, CELLS * 2 * L, total)
    for c in range(n_col):
        at = n_row * 2 * L + c * L
        value = cols[c] + recv[at:at + L, :].astype(F32)
        slot, inner = c // CELLS, c % CELLS
        to = (slot // 2) * CELLS + inner
        if slot % 2 == 0:
            cols_out[to] = value
        else:
            y_msg[to * L:(to + 1) * L, :] = value.astype(BF16)
    put_split(y_msg, steps * CELLS * L, total)


def near_sum(chips, steps, *refs):
    x_in, refs = refs[:chips - 1], refs[chips - 1:]
    xy_in, refs = refs[:chips - 1], refs[chips - 1:]
    (y_in, rows, cols, par), refs = refs[:4], refs[4:]
    rows_out, cols_out, par_out = refs[:3]
    z_msgs = refs[3:]
    total = par[...] + get_split(y_in, steps * CELLS * L, HALF)
    for ref in x_in:
        total = total + get_split(ref, CELLS * 2 * L, HALF)
    for ref in xy_in:
        total = total + get_split(ref, 0, HALF)
    par_out[...] = total
    for c in range(CELLS):
        value = rows[c]
        for ref in x_in:
            value = value + ref[c * 2 * L:(c + 1) * 2 * L, :].astype(F32)
        rows_out[c] = value
    for c in range(steps * CELLS):
        value = cols[c] + y_in[c * L:(c + 1) * L, :].astype(F32)
        step, inner = c // CELLS, c % CELLS
        if step == 0:
            cols_out[inner] = value
        else:
            z_msgs[step - 1][inner * L:(inner + 1) * L, :] = value.astype(BF16)
    for ref in z_msgs:
        ref[CELLS * L:, :] = total.astype(BF16)


def far_par(steps, *refs):
    z_in, (par, par_out) = refs[:steps - 1], refs[steps - 1:]
    total = par[...]
    for ref in z_in:
        total = total + ref[CELLS * L:, :].astype(F32)
    par_out[...] = total


def far_cells(steps, *refs):
    z_in, refs = refs[:steps - 1], refs[steps - 1:]
    rows, cols, own, updated, grad_feats = refs
    for c in range(CELLS):
        value = cols[c]
        for ref in z_in:
            value = value + ref[c * L:(c + 1) * L, :].astype(F32)
        updated[c] = (own[c, 0:L, :].astype(F32) + rows[c, :L, :]).astype(BF16)
        grad_feats[c] = own[c, L:2 * L, :].astype(F32) + rows[c, L:, :] + value


def gather_halves(own, oth, first, bias1, dist, second, bias2, par):
    core = lax.rem(lax.axis_index("col"), 2)
    par[pl.ds(pl.multiple_of(core * HALF, HALF), HALF), :] = own[...]
    par[pl.ds(pl.multiple_of((1 - core) * HALF, HALF), HALF), :] = oth[...]
    first[...] = jnp.transpose(par[:2 * L, :])
    second[...] = par[2 * L:3 * L, :]
    bias1[...] = par[3 * L:3 * L + 1, :]
    dist[...] = par[3 * L + 1:3 * L + 2, :]
    bias2[...] = par[3 * L + 2:3 * L + 3, :L]


def per_device(
    feats, coords, valid, pairs, pair_count, w_first, bias_first, dist_scale,
    w_second, bias_second, cotangent, rows_n, cols_n,
):
    steps, chips = rows_n // 2, cols_n // 2
    swap_y = [(i, i ^ 1) for i in range(rows_n)]
    swap_core = [(i, i ^ 1) for i in range(cols_n)]

    def along(n, d):
        return [(i, (i + 2 * d) % n) for i in range(n)]

    def diagonal(d):
        return [
            (r * cols_n + c, (r ^ 1) * cols_n + (c + 2 * d) % cols_n)
            for r in range(rows_n) for c in range(cols_n)
        ]

    spot = lax.broadcasted_iota(jnp.int32, (CELLS, GROUP, CP), 1)
    extra = jnp.where(
        spot == 3, valid.astype(BF16)[:, None, :], jnp.pad(coords, ((0, 0), (0, GROUP - 3), (0, 0)))
    )
    col_own = jnp.concatenate([feats, extra], axis=1)
    col_own, late = lax.optimization_barrier((col_own, cotangent))
    row_own = jnp.concatenate([col_own[:, :L], late, col_own[:, L:]], axis=1)
    tiles = jnp.concatenate([pairs.reshape(-1), pair_count.reshape(-1)])
    vectors = jnp.stack([bias_first, dist_scale, jnp.pad(bias_second, (0, L)), bias_first])
    col_y = lax.ppermute(col_own, "row", swap_y)
    col_y, vectors = lax.optimization_barrier((col_y, vectors))
    col_pair = jnp.concatenate([col_own, col_y], axis=0)
    row_parts = [row_own] + [
        lax.ppermute(row_own, "col", along(cols_n, -d)) for d in range(1, chips)
    ]
    col_parts = [col_pair] + [
        lax.ppermute(col_pair, "row", along(rows_n, -d)) for d in range(1, steps)
    ]
    other_tiles = lax.ppermute(tiles, "col", swap_core)
    row_swapped = [lax.ppermute(p, "col", swap_core) for p in row_parts]
    col_parts[-1], other_tiles, *row_swapped = lax.optimization_barrier(
        (col_parts[-1], other_tiles, *row_swapped)
    )
    row_parts += row_swapped
    col_parts += [lax.ppermute(p, "col", swap_core) for p in col_parts]
    send, rows, cols, par = pair_call(
        [tiles, other_tiles], row_parts, col_parts,
        [w_first, w_second, vectors],
    )
    got = lax.ppermute(send, "col", swap_core)
    x_shape = ((CELLS * 2 * L + PAR, CP), BF16)
    keep = [((CELLS, 2 * L, CP), F32), ((steps * CELLS, L, CP), F32), ((HALF, H), F32)]
    outs = call(
        functools.partial(core_sum, chips, steps), "core_sum", [got, rows, cols, par],
        [x_shape] * (chips - 1)
        + [((steps * CELLS * L + PAR, CP), BF16), ((PAR, H), BF16)] + keep,
    )
    x_msgs, (y_msg, xy_msg, rows, cols, par) = outs[:chips - 1], outs[chips - 1:]
    y_in = lax.ppermute(y_msg, "row", swap_y)
    x_in = [lax.ppermute(m, "col", along(cols_n, d + 1)) for d, m in enumerate(x_msgs)]
    xy_in = [lax.ppermute(xy_msg, ("row", "col"), diagonal(d)) for d in range(1, chips)]
    keep[1] = ((CELLS, L, CP), F32)
    rows, cols, par, *z_msgs = call(
        functools.partial(near_sum, chips, steps), "near_sum",
        [*x_in, *xy_in, y_in, rows, cols, par],
        keep + [((CELLS * L + HALF, CP), BF16)] * (steps - 1),
    )
    z_in = [lax.ppermute(m, "row", along(rows_n, d + 1)) for d, m in enumerate(z_msgs)]
    par, = call(
        functools.partial(far_par, steps), "far_par", [*z_in, par], [((HALF, H), F32)], limit=16
    )
    par_in = lax.ppermute(par, "col", swap_core)
    updated, grad_feats = call(
        functools.partial(far_cells, steps), "far_cells",
        [*z_in, rows, cols, row_own],
        [((CELLS, L, CP), BF16), ((CELLS, L, CP), F32)], limit=16,
    )
    first, bias1, dist, second, bias2 = call(
        gather_halves, "gather_halves", [par, par_in],
        [((H, 2 * L), F32), ((1, H), F32), ((1, H), F32), ((L, H), F32), ((1, L), F32)],
        [pltpu.VMEM((PAR, H), F32)],
    )
    return updated, grad_feats, first, bias1[0], dist[0], second, bias2[0]


def solution(mesh):
    spread = P(("row", "col"))
    placed = (spread, spread, spread, P("row", "col"), P("row", "col"), P(), P(), P(), P(), P(), spread)
    return jax.shard_map(
        functools.partial(per_device, rows_n=mesh.shape["row"], cols_n=mesh.shape["col"]),
        mesh=mesh,
        in_specs=placed,
        out_specs=(spread, spread, P(), P(), P(), P(), P()),
        check_vma=False,
    )
```
